32 devices in a mesh: job: 2 (over y), aux: 16 (over z, x, core).
Axes of the slice: x: 2, y: 2, z: 4, core: 2. Of those that a mesh axis runs over, the one named last changes fastest.
Arguments:
- ints_ov: bfloat16 [256, 384, 384], P(('job', 'aux')), parts along dimension 0, may hold values from -0.3125 to 0.3125
- ints_oo: bfloat16 [256, 2, 384], P(('job', 'aux')), parts along dimension 0, may hold values from -1.5 to 1.5
- trial: bfloat16 [64, 4, 384], P('job'), parts along dimension 0, may hold values from -6 to 6
- occ_energy: float32 [64], P('job'), parts along dimension 0, may hold values from -1 to -0.2
- vir_energy: float32 [32000], P('job'), parts along dimension 0, may hold values from 0.2 to 2.5
- root_shift: float32 [8], P('job'), parts along dimension 0, may hold values from 0.1 to 0.6
- vir_blocks: int32 [32, 3], P('job'), parts along dimension 0, may hold values from 0 to 124, as said below
- pair_list: int32 [32, 4, 2], P('job'), parts along dimension 0, may hold values from 0 to 31, as said below
- pair_count: int32 [32], P('job'), parts along dimension 0, may hold values from 2 to 4, as said below
Outputs:
- sigma: float32 [64, 4, 384], P(('job', 'aux')), parts along dimension 0
The draws below stay inside these ranges and needn't reach their ends.
There are 2 independent parts, one for each index of `job`. The reference program is written for one: setup_inputs(seed, part) draws one part's arguments, and reference() takes and returns one part's arrays. A program takes and returns all parts, laid end to end along the dimension named above; each array names one. Nothing has to cross between parts.
Inputs may be any that keep to these rules, and one draw needn't show every extreme that they name: `pair_count`: some domain has 4 live pairs. `pair_list`: for domain d all 4 slots hold distinct pairs (i, j): i an occupied of domain d (d * 2 to d * 2 + 1) and j an occupied of one of the domains d + 1 to d + 3, taken cyclically modulo 16; slots from pair_count[d] on are not live. `vir_blocks`: the blocks of one domain are distinct.
All inputs are finite; a program needn't handle non-finite values.
Results may differ from the reference program's by a relative error of at most 0.00036.
Values may be sent and summed in bfloat16 or wider, within the bound.
No kernel may reach another device: no remote copies, remote signals or barrier semaphores. Data moves between devices by JAX's collectives and lax.ppermute only.
A program may use at most 128 MiB of HBM per device.

```python
import math
import jax
import jax.numpy as jnp
from jax import lax

FB = 384
DV = 384
NV = 16000
K = 4
OD = 2
NN = 4
PMAX = 4
NDOM = 16
OCC = 32
SLAB = 8


def pair_tables(key):
    base_key = jax.random.fold_in(key, 7001)
    uniform_ints = jax.random.randint(jax.random.fold_in(base_key, 1), (NDOM,), 0, 16)
    counts = 2 + (uniform_ints >= 10).astype(jnp.int32) + (uniform_ints >= 14).astype(jnp.int32)
    counts = jnp.minimum(counts, PMAX)
    busiest = jax.random.randint(jax.random.fold_in(base_key, 2), (), 0, NDOM)
    domains = jnp.arange(NDOM, dtype=jnp.int32)
    counts = jnp.where(domains == busiest, PMAX, counts).astype(jnp.int32)
    options = OD * OD * (NN - 1)
    domain_keys = jax.random.split(jax.random.fold_in(base_key, 3), NDOM)
    chosen = jax.vmap(lambda one_key: jax.random.permutation(one_key, options)[:PMAX])(domain_keys).astype(jnp.int32)
    per_side = (NN - 1) * OD
    own_slot = chosen // per_side
    remainder = chosen % per_side
    ahead_by = 1 + remainder // OD
    other_slot = remainder % OD
    occ_first = domains[:, None] * OD + own_slot
    occ_second = (domains[:, None] + ahead_by) % NDOM * OD + other_slot
    return (counts, jnp.stack([occ_first, occ_second], axis=-1).astype(jnp.int32))


def draw_pair_list(key, part):
    return pair_tables(key)[1]


def draw_pair_count(key, part):
    return pair_tables(key)[0]


def draw_vir_blocks(key, part):
    domain_keys = jax.random.split(jax.random.fold_in(key, 9001), NDOM)
    chosen = jax.vmap(lambda one_key: jax.random.permutation(one_key, NV // 128)[:DV // 128])(domain_keys)
    return chosen.astype(jnp.int32)


def block_levels(own_key, shape, cuts, least, largest):
    gain, own = 1.0, jax.random.fold_in(own_key, 6)
    for axis_at, blocks in cuts:
        heights = jnp.exp(jax.random.uniform(jax.random.fold_in(own, axis_at), (blocks,), jnp.float32, least / len(cuts), largest / len(cuts)))
        gain = gain * jnp.repeat(heights, shape[axis_at] // blocks).reshape([-1 if axis == axis_at else 1 for axis in range(len(shape))])
    return gain


def noise(key, shape, width, most, shards=(), kind=jnp.bfloat16):
    factor_of = block_levels(key, shape, shards, -0.22, 0.18) if shards else 1.0
    array = jax.random.normal(key, shape, jnp.float32) * width * factor_of
    return jnp.minimum(jnp.maximum(array, -most), most).astype(kind)


def setup_inputs(seed: int = 0, part: int = 0) -> dict:
    arg_keys = jax.random.split(jax.random.key(seed), 10)
    own_keys = jax.random.split(jax.random.fold_in(arg_keys[9], part), 10)
    ints_ov = noise(own_keys[0], (NDOM * SLAB, FB, DV), FB ** -0.5, 0.3125, ((0, 16),))
    ints_oo = noise(own_keys[1], (NDOM * SLAB, OD, FB), 0.25, 1.5, ((0, 16),))
    trial = noise(own_keys[2], (OCC, K, DV), 1.0, 6.0)
    occ_energy = jnp.clip(jax.random.uniform(own_keys[3], (OCC,), jnp.float32, -1.0, -0.2), -1.0, -0.2)
    vir_energy = jnp.clip(jnp.exp(jax.random.uniform(own_keys[4], (NV,), jnp.float32, math.log(0.2), math.log(2.5))), 0.2, 2.5)
    root_shift = jnp.clip(jax.random.uniform(own_keys[5], (K,), jnp.float32, 0.1, 0.6), 0.1, 0.6)
    vir_blocks = draw_vir_blocks(jax.random.fold_in(jax.random.fold_in(arg_keys[9], part), 71), part)
    pair_list = draw_pair_list(jax.random.fold_in(jax.random.fold_in(arg_keys[9], part), 71), part)
    pair_count = draw_pair_count(jax.random.fold_in(jax.random.fold_in(arg_keys[9], part), 71), part)
    return dict(ints_ov=ints_ov, ints_oo=ints_oo, trial=trial, occ_energy=occ_energy, vir_energy=vir_energy, root_shift=root_shift, vir_blocks=vir_blocks, pair_list=pair_list, pair_count=pair_count)


def product(pattern, left_arg, right_arg):
    return jnp.einsum(pattern, left_arg.astype(jnp.float32), right_arg.astype(jnp.float32))


def reference(ints_ov, ints_oo, trial, occ_energy, vir_energy, root_shift, vir_blocks, pair_list, pair_count):
    slab_table = ints_ov.reshape(NDOM, SLAB, FB, DV)
    coupling_table = ints_oo.reshape(NDOM, SLAB, OD, FB)
    level_table = vir_energy.reshape(NV // 128, 128)

    def levels(domain):
        return jnp.take(level_table, vir_blocks[domain], axis=0).reshape(DV)

    def dressed(coupling, domain):
        occupied = lax.dynamic_slice_in_dim(trial, (domain * OD).astype(jnp.int32), OD, 0)
        return (-product("lq,lka->kqa", coupling, occupied)).astype(jnp.bfloat16)

    def deposit(accum_sigma, contribution, domain):
        start_row = (domain * OD).astype(jnp.int32)
        current = lax.dynamic_slice_in_dim(accum_sigma, start_row, OD, 0)
        return lax.dynamic_update_slice_in_dim(accum_sigma, current + contribution, start_row, 0)

    def visit(accum_sigma, flat_index):
        domain = flat_index // PMAX
        position = flat_index % PMAX
        occ_first = pair_list[domain, position, 0]
        occ_second = pair_list[domain, position, 1]
        partner = occ_second // OD
        row_first = occ_first - domain * OD
        row_second = ((partner - domain) % NDOM) * OD + occ_second % OD

        def pair_step(running):
            b_first = slab_table[domain, row_first]
            b_second = slab_table[domain, row_second]
            c_first = coupling_table[domain, row_first]
            c_second = coupling_table[domain, row_second]
            z_first = dressed(c_first, domain)
            z_second = dressed(c_second, partner)
            coupled = product("kqa,qb->kab", z_first, b_second) + product("qa,kqb->kab", b_first, z_second)
            denominator = levels(domain)[None, :, None] + levels(partner)[None, None, :] - occ_energy[occ_first] - occ_energy[occ_second] - root_shift[:, None, None]
            doubles = (coupled / denominator).astype(jnp.bfloat16)
            gamma_first = product("kab,qb->kqa", doubles, b_second).astype(jnp.bfloat16)
            gamma_second = product("kab,qa->kqb", doubles, b_first).astype(jnp.bfloat16)
            sigma_first = -product("lq,kqa->lka", c_first, gamma_first)
            sigma_second = -product("lq,kqb->lkb", c_second, gamma_second)
            running = deposit(running, sigma_first, domain)
            return deposit(running, sigma_second, partner)

        accum_sigma = lax.cond(pair_count[domain] > position, pair_step, lambda unchanged: unchanged, accum_sigma)
        return accum_sigma, None

    initial = jnp.zeros((OCC, K, DV), jnp.float32)
    accum_sigma, _ = lax.scan(visit, initial, jnp.arange(NDOM * PMAX, dtype=jnp.int32))
    return accum_sigma
```

```python
import functools

import jax
import jax.numpy as jnp
from jax import lax
from jax.experimental import pallas as pl
from jax.experimental.pallas import tpu as pltpu
from jax.sharding import PartitionSpec as P

F32, BF16 = jnp.float32, jnp.bfloat16
LANES = 128


def passed_along(value, axis, steps):
    count = lax.axis_size(axis)
    pairs = [(source, (source + steps) % count) for source in range(count)]
    return lax.ppermute(value, axis, pairs)


def high_low(value):
    high = value.astype(BF16).astype(F32)
    return high, (value - high).astype(BF16).astype(F32)


def pair_of(pairs, slot, me, ndomain, od):
    first, second = pairs[me, slot, 0], pairs[me, slot, 1]
    partner = lax.div(second, od)
    ahead = lax.rem(partner - me + ndomain, ndomain)
    return first, second, partner, ahead, first - me * od, ahead * od + lax.rem(second, od)


def levels_of(vir, blocks, domain):
    return jnp.concatenate(
        [vir[pl.ds(blocks[domain, part], 1), :] for part in range(blocks.shape[1])], axis=1
    )


def column(row):
    return jnp.concatenate(
        [
            jnp.broadcast_to(row[:, at : at + LANES], (LANES, LANES)).T
            for at in range(0, row.shape[1], LANES)
        ],
        axis=0,
    )


def half_pair(roots, od, x_trial, x_w, y_trial, y_w, x_levels, y_levels, shifts, dot_w):
    width = y_levels.shape[1]
    x_high, x_low = high_low(x_w)
    y_high, y_low = high_low(y_w)
    n_trial = roots * od
    rows = 2 * n_trial + 2 * od
    pad = -rows % 16
    blank = [jnp.zeros((pad, width), F32)] if pad else []
    x_mat = jnp.concatenate([x_trial, x_trial, x_high, x_low] + blank, axis=0).T.astype(BF16)
    d_high, d_low = high_low(dot_w)
    left = jnp.concatenate([d_high, d_low, jnp.zeros((16 - 2 * od, width), F32)], axis=0).astype(BF16)
    results = []
    for k in range(roots):
        before = [jnp.zeros((k * od, width), F32)] if k else []
        after = [jnp.zeros(((roots - 1 - k) * od, width), F32)] if k < roots - 1 else []
        mine = y_trial[k * od : (k + 1) * od]
        y_mat = jnp.concatenate(
            before + [y_high] + after + before + [y_low] + after + [mine, mine] + blank, axis=0
        ).astype(BF16)
        coupled = jnp.dot(x_mat, y_mat, preferred_element_type=F32)
        y_shifted = y_levels - shifts[k]
        denominator = jnp.concatenate([x_levels] * (width // LANES), axis=1) + y_shifted
        doubles = (coupled * pl.reciprocal(denominator, approx=True)).astype(BF16)
        both = jnp.dot(left, doubles, preferred_element_type=F32)
        results.append(both[:od] + both[od : 2 * od])
    return results


def trial_rows(trial, domain, od):
    by_occ = [trial[domain * od + l].astype(F32) for l in range(od)]
    roots = by_occ[0].shape[0]
    return jnp.concatenate([by_occ[l][k : k + 1] for k in range(roots) for l in range(od)], axis=0)


def send_kernel(
    ndomain, pairs, counts, blocks, occ, shift, ints, couple, trial, vir, *rest
):
    *sends, weights, total, x_levels = rest
    slab, od, fit = couple.shape
    roots, width = trial.shape[1:]
    me = lax.axis_index("aux")
    couplings = jnp.concatenate([couple[row].astype(F32) for row in range(slab)], axis=0).astype(BF16)
    for row in range(slab):
        found = jnp.dot(couplings, ints[row], preferred_element_type=F32)
        for other in range(od, slab) if row < od else range(od):
            weights[row, other] = found[other * od : (other + 1) * od]
    total[...] = jnp.zeros_like(total)
    x_levels[...] = column(levels_of(vir, blocks, me))
    mine = trial_rows(trial, me, od)

    @pl.loop(0, counts[me])
    def _(slot):
        first, second, partner, ahead, row_i, row_j = pair_of(pairs, slot, me, ndomain, od)
        w_i = weights[row_i, row_j]
        w_j = weights[row_j, row_i]
        shifts = [occ[first] + occ[second] + shift[k] for k in range(roots)]
        found = half_pair(
            roots, od, mine, w_i, trial_rows(trial, partner, od), w_j,
            x_levels[...], levels_of(vir, blocks, partner), shifts, w_i,
        )
        for l in range(od):
            total[ahead, l] += jnp.concatenate([found[k][l : l + 1] for k in range(roots)], axis=0)

    for ahead, send in enumerate(sends):
        send[...] = total[ahead + 1]


def keep_kernel(ndomain, pairs, counts, blocks, occ, shift, weights, trial, vir, kept):
    slab = weights.shape[0]
    roots, width = trial.shape[1:]
    od = weights.shape[2]
    me = lax.axis_index("aux")
    kept[...] = jnp.zeros_like(kept)
    mine = trial_rows(trial, me, od)
    my_levels = levels_of(vir, blocks, me)

    @pl.loop(0, counts[me])
    def _(slot):
        first, second, partner, ahead, row_i, row_j = pair_of(pairs, slot, me, ndomain, od)
        w_i = weights[row_i, row_j]
        w_j = weights[row_j, row_i]
        shifts = [occ[first] + occ[second] + shift[k] for k in range(roots)]
        found = half_pair(
            roots, od, trial_rows(trial, partner, od), w_j, mine, w_i,
            column(levels_of(vir, blocks, partner)), my_levels, shifts, w_j,
        )
        for l in range(od):
            kept[l] += jnp.concatenate([found[k][l : l + 1] for k in range(roots)], axis=0)


def per_device(
    ints_ov, ints_oo, trial, occ_energy, vir_energy, root_shift, vir_blocks, pair_list, pair_count
):
    slab, od, fit = ints_oo.shape
    roots, width = trial.shape[1:]
    ndomain = lax.axis_size("aux")
    span = slab // od
    level_table = vir_energy.reshape(-1, LANES)
    smem = pl.BlockSpec(memory_space=pltpu.SMEM)
    vmem = pl.BlockSpec(memory_space=pltpu.VMEM)
    part = jax.ShapeDtypeStruct((od, roots, width), F32)
    params = pltpu.CompilerParams(vmem_limit_bytes=48 * 1024 * 1024)
    *sends, weights = pl.pallas_call(
        functools.partial(send_kernel, ndomain),
        out_shape=[part] * (span - 1) + [jax.ShapeDtypeStruct((slab, slab, od, width), F32)],
        in_specs=[smem] * 5 + [vmem] * 4,
        out_specs=[vmem] * span,
        scratch_shapes=[
            pltpu.VMEM((span, od, roots, width), F32),
            pltpu.VMEM((width, LANES), F32),
        ],
        compiler_params=params,
        name="to_send",
    )(pair_list, pair_count, vir_blocks, occ_energy, root_shift, ints_ov, ints_oo, trial, level_table)
    arrived = [passed_along(send, "aux", at + 1) for at, send in enumerate(sends)]
    kept = pl.pallas_call(
        functools.partial(keep_kernel, ndomain),
        out_shape=part,
        in_specs=[smem] * 5 + [vmem] * 3,
        out_specs=vmem,
        compiler_params=params,
        cost_estimate=pl.CostEstimate(flops=10**9, bytes_accessed=10**6, transcendentals=10**6),
        name="to_keep",
    )(pair_list, pair_count, vir_blocks, occ_energy, root_shift, weights, trial, level_table)
    return functools.reduce(jnp.add, arrived, kept)


def solution(mesh):
    in_specs = (
        P(("job", "aux"), None, None),
        P(("job", "aux"), None, None),
        P("job", None, None),
        P("job"),
        P("job"),
        P("job"),
        P("job", None),
        P("job", None, None),
        P("job"),
    )
    out_specs = P(("job", "aux"), None, None)
    return jax.shard_map(
        per_device, mesh=mesh, in_specs=in_specs, out_specs=out_specs, check_vma=False
    )
```

```python
import functools

import jax
import jax.numpy as jnp
from jax import lax
from jax.experimental import pallas as pl
from jax.experimental.pallas import tpu as pltpu
from jax.sharding import PartitionSpec as P

F32, BF16 = jnp.float32, jnp.bfloat16
LANES = 128


def passed_along(value, axis, steps):
    count = lax.axis_size(axis)
    pairs = [(source, (source + steps) % count) for source in range(count)]
    return lax.ppermute(value, axis, pairs)


def pair_of(pairs, slot, me, ndomain, od):
    first, second = pairs[slot, 0, me], pairs[slot, 1, me]
    partner = lax.div(second, od)
    ahead = lax.rem(partner - me + ndomain, ndomain)
    return first, second, ahead, first - me * od, ahead * od + lax.rem(second, od)


def column(row):
    return jnp.concatenate(
        [
            jnp.broadcast_to(row[:, at : at + LANES], (LANES, LANES)).T
            for at in range(0, row.shape[1], LANES)
        ],
        axis=0,
    )


def spread(w, roots):
    return jnp.concatenate(
        [jnp.broadcast_to(w[l : l + 1], (roots, w.shape[1])) for l in range(w.shape[0])], axis=0
    )


def factors(trial, w, roots):
    od, width = w.shape
    by_trial = [
        jnp.concatenate([trial[l * roots : (l + 1) * roots]] * od, axis=0) for l in range(od)
    ]
    by_w = [jnp.broadcast_to(w[l : l + 1], (od * roots, width)) for l in range(od)]
    return by_trial, by_w


def half_pair(roots, x_trial, x_w, y_trial, y_w, x_levels, y_levels, shifts):
    od, width = x_w.shape
    rows = od * roots
    x_by_trial, x_by_w = factors(x_trial, x_w, roots)
    y_by_trial, y_by_w = factors(y_trial, y_w, roots)
    weight = spread(x_w, roots)
    left = jnp.concatenate([part * weight for part in x_by_trial + x_by_w], axis=0)
    high = left.astype(BF16).astype(F32)
    left = jnp.concatenate([high, left - high], axis=0)
    root_of = lax.rem(lax.broadcasted_iota(jnp.int32, left.shape, 0), roots)
    summed = jnp.zeros((left.shape[0], width), F32)
    x_wide = jnp.concatenate([x_levels] * (width // LANES), axis=1)
    for k in range(roots):
        inverse = pltpu.reciprocal(x_wide + (y_levels - shifts[k]), approx=True).astype(BF16)
        mine = jnp.where(root_of == k, left, 0.0).astype(BF16)
        summed += jnp.dot(mine, inverse, preferred_element_type=F32)
    half = summed.shape[0] // 2
    summed = summed[:half] + summed[half:]
    parts = [
        summed[at * rows : (at + 1) * rows] * other for at, other in enumerate(y_by_w + y_by_trial)
    ]
    return functools.reduce(jnp.add, parts)


def send_kernel(
    ndomain, pairs_hbm, counts_hbm, blocks_hbm, occ_hbm, shift_hbm, ints_hbm, couple_hbm, trial_hbm, vir_hbm,
    *rest,
):
    slab, od, fit = couple_hbm.shape
    roots, width = trial_hbm.shape[1:]
    span = slab // od
    sends, rest = rest[: span - 1], rest[span - 1 :]
    (weights, trials, levels, pairs, counts, blocks, occ, shift, ints, couple, trial, vir, total, x_levels, sems) = rest
    me = lax.axis_index("aux")
    small = [
        pltpu.make_async_copy(source, target, sems.at[at])
        for at, (source, target) in enumerate(
            [
                (blocks_hbm, blocks), (pairs_hbm, pairs), (counts_hbm, counts), (occ_hbm, occ),
                (shift_hbm, shift), (vir_hbm, vir), (couple_hbm, couple),
            ]
        )
    ]
    at = len(small)
    near = [lax.rem(me + ahead, ndomain) for ahead in range(span)]
    some_trial = [
        pltpu.make_async_copy(
            trial_hbm.at[pl.ds(near[ahead] * od, od)], trial.at[ahead], sems.at[at + ahead]
        )
        for ahead in range(span)
    ]
    at += span
    big = [
        pltpu.make_async_copy(ints_hbm.at[row], ints.at[row], sems.at[at + row]) for row in range(slab)
    ]
    for copy in small + some_trial + big:
        copy.start()
    total[...] = jnp.zeros_like(total)
    for copy in small:
        copy.wait()
    for ahead in range(span):
        row = jnp.concatenate(
            [vir[pl.ds(blocks[part, near[ahead]], 1), :] for part in range(blocks.shape[0])], axis=1
        )
        levels[ahead] = row
        if ahead == 0:
            x_levels[...] = column(row)
    for ahead in range(span):
        some_trial[ahead].wait()
        trials[ahead] = jnp.concatenate([trial[ahead, l].astype(F32) for l in range(od)], axis=0)
    couplings = jnp.concatenate([couple[row].astype(F32) for row in range(slab)], axis=0).astype(BF16)
    for row in range(slab):
        big[row].wait()
        found = jnp.dot(couplings, ints[row], preferred_element_type=F32)
        for other in range(od, slab) if row < od else range(od):
            weights[row, other] = found[other * od : (other + 1) * od]

    @pl.loop(0, counts[me])
    def _(slot):
        first, second, ahead, row_i, row_j = pair_of(pairs, slot, me, ndomain, od)
        total[ahead] += half_pair(
            roots, trials[0], weights[row_i, row_j], trials[ahead], weights[row_j, row_i],
            x_levels[...], levels[ahead], [occ[first] + occ[second] + shift[k] for k in range(roots)],
        )

    for ahead, send in enumerate(sends):
        for l in range(od):
            send[l] = total[ahead + 1, l * roots : (l + 1) * roots]


def keep_kernel(
    ndomain, pairs_hbm, counts_hbm, occ_hbm, shift_hbm, weights, trials, levels, kept,
    pairs, counts, occ, shift, total, x_levels, sems,
):
    span, rows, width = trials.shape
    od = weights.shape[2]
    roots = rows // od
    me = lax.axis_index("aux")
    small = [
        pltpu.make_async_copy(source, target, sems.at[at])
        for at, (source, target) in enumerate(
            [(pairs_hbm, pairs), (counts_hbm, counts), (occ_hbm, occ), (shift_hbm, shift)]
        )
    ]
    for copy in small:
        copy.start()
    total[...] = jnp.zeros_like(total)
    for ahead in range(span):
        x_levels[ahead] = column(levels[ahead])
    for copy in small:
        copy.wait()

    @pl.loop(0, counts[me])
    def _(slot):
        first, second, ahead, row_i, row_j = pair_of(pairs, slot, me, ndomain, od)
        total[...] += half_pair(
            roots, trials[ahead], weights[row_j, row_i], trials[0], weights[row_i, row_j],
            x_levels[ahead], levels[0], [occ[first] + occ[second] + shift[k] for k in range(roots)],
        )

    for l in range(od):
        kept[l] = total[l * roots : (l + 1) * roots]


def per_device(
    ints_ov, ints_oo, trial, occ_energy, vir_energy, root_shift, vir_blocks, pair_list, pair_count
):
    slab, od, fit = ints_oo.shape
    roots, width = trial.shape[1:]
    ndomain = lax.axis_size("aux")
    span = slab // od
    level_table = vir_energy.reshape(-1, LANES)
    pairs = jnp.transpose(pair_list, (1, 2, 0))
    blocks = vir_blocks.T
    hbm = pl.BlockSpec(memory_space=pltpu.HBM)
    vmem = pl.BlockSpec(memory_space=pltpu.VMEM)
    part = jax.ShapeDtypeStruct((od, roots, width), F32)
    params = pltpu.CompilerParams(vmem_limit_bytes=40 * 1024 * 1024)
    scalars = [pltpu.SMEM(x.shape, x.dtype) for x in (pairs, pair_count, blocks, occ_energy, root_shift)]
    def stay(*arrays):
        return [pltpu.with_memory_space_constraint(array, pltpu.HBM) for array in arrays]

    *sends, weights, trials, levels = pl.pallas_call(
        functools.partial(send_kernel, ndomain),
        out_shape=[part] * (span - 1)
        + [
            jax.ShapeDtypeStruct((slab, slab, od, width), F32),
            jax.ShapeDtypeStruct((span, od * roots, width), F32),
            jax.ShapeDtypeStruct((span, 1, width), F32),
        ],
        in_specs=[hbm] * 9,
        out_specs=[vmem] * (span + 2),
        scratch_shapes=scalars
        + [
            pltpu.VMEM(ints_ov.shape, BF16),
            pltpu.VMEM(ints_oo.shape, BF16),
            pltpu.VMEM((span, od, roots, width), BF16),
            pltpu.VMEM(level_table.shape, F32),
            pltpu.VMEM((span, od * roots, width), F32),
            pltpu.VMEM((width, LANES), F32),
            pltpu.SemaphoreType.DMA((7 + span + slab,)),
        ],
        compiler_params=params,
        name="to_send",
    )(*stay(pairs, pair_count, blocks, occ_energy, root_shift, ints_ov, ints_oo, trial, level_table))
    arrived = [passed_along(send, "aux", at + 1) for at, send in enumerate(sends)]
    kept = pl.pallas_call(
        functools.partial(keep_kernel, ndomain),
        out_shape=part,
        in_specs=[hbm] * 4 + [vmem] * 3,
        out_specs=vmem,
        scratch_shapes=scalars[:2]
        + scalars[3:]
        + [
            pltpu.VMEM((od * roots, width), F32),
            pltpu.VMEM((span, width, LANES), F32),
            pltpu.SemaphoreType.DMA((4,)),
        ],
        compiler_params=params,
        cost_estimate=pl.CostEstimate(flops=10**9, bytes_accessed=10**6, transcendentals=10**6),
        name="to_keep",
    )(*stay(pairs, pair_count, occ_energy, root_shift), weights, trials, levels)
    return functools.reduce(jnp.add, arrived, kept)


def solution(mesh):
    in_specs = (
        P(("job", "aux"), None, None),
        P(("job", "aux"), None, None),
        P("job", None, None),
        P("job"),
        P("job"),
        P("job"),
        P("job", None),
        P("job", None, None),
        P("job"),
    )
    out_specs = P(("job", "aux"), None, None)
    return jax.shard_map(
        per_device, mesh=mesh, in_specs=in_specs, out_specs=out_specs, check_vma=False
    )
```

```python
import functools

import jax
import jax.numpy as jnp
from jax import lax
from jax.experimental import pallas as pl
from jax.experimental.pallas import tpu as pltpu
from jax.sharding import PartitionSpec as P

F32, BF16 = jnp.float32, jnp.bfloat16
LANES = 128


def passed_along(value, axis, steps):
    count = lax.axis_size(axis)
    pairs = [(source, (source + steps) % count) for source in range(count)]
    return lax.ppermute(value, axis, pairs)


def column(row):
    return jnp.concatenate(
        [
            jnp.broadcast_to(row[:, at : at + LANES], (LANES, LANES)).T
            for at in range(0, row.shape[1], LANES)
        ],
        axis=0,
    )


def spread(w, roots):
    return jnp.concatenate(
        [jnp.broadcast_to(w[l : l + 1], (roots, w.shape[1])) for l in range(w.shape[0])], axis=0
    )


def factors(trial, w, roots):
    od, width = w.shape
    by_trial = [
        jnp.concatenate([trial[l * roots : (l + 1) * roots]] * od, axis=0) for l in range(od)
    ]
    by_w = [jnp.broadcast_to(w[l : l + 1], (od * roots, width)) for l in range(od)]
    return by_trial, by_w


def root_shifts(pairs, occ, shift, slot, me, roots):
    energy = occ[pairs[slot, 0, me]] + occ[pairs[slot, 1, me]]
    return [energy + shift[k] for k in range(roots)]


def invert(target, x_levels, y_levels, shifts, step=64):
    width = y_levels.shape[1]
    roots = len(shifts)
    for k in range(0, roots, 2):
        for at in range(0, width, step):
            x_wide = jnp.concatenate([x_levels[at : at + step]] * (width // LANES), axis=1)
            one = x_wide + (y_levels - shifts[k])
            if k + 1 == roots:
                found = [pltpu.reciprocal(one, approx=True)]
            else:
                two = x_wide + (y_levels - shifts[k + 1])
                both = pltpu.reciprocal(one * two, approx=True)
                found = [both * two, both * one]
            for more, value in enumerate(found):
                start = (k + more) * width + at
                target[start : start + step] = value.astype(BF16)


def contract(roots, x_trial, x_w, y_trial, y_w, inverse):
    od, width = x_w.shape
    rows = od * roots
    x_by_trial, x_by_w = factors(x_trial, x_w, roots)
    y_by_trial, y_by_w = factors(y_trial, y_w, roots)
    weight = spread(x_w, roots)
    left = jnp.concatenate([part * weight for part in x_by_trial + x_by_w], axis=0)
    high = left.astype(BF16).astype(F32)
    left = jnp.concatenate([high, left - high], axis=0)
    root_of = lax.rem(lax.broadcasted_iota(jnp.int32, left.shape, 0), roots)
    left = jnp.concatenate(
        [jnp.where(root_of == k, left, 0.0).astype(BF16) for k in range(roots)], axis=1
    )
    summed = jnp.dot(left, inverse, preferred_element_type=F32)
    half = summed.shape[0] // 2
    summed = summed[:half] + summed[half:]
    parts = [
        summed[at * rows : (at + 1) * rows] * other for at, other in enumerate(y_by_w + y_by_trial)
    ]
    return functools.reduce(jnp.add, parts)


def send_kernel(
    ndomain, sure, pairs_hbm, counts_hbm, blocks_hbm, occ_hbm, shift_hbm, ints_hbm, couple_hbm, trial_hbm, vir_hbm,
    *rest,
):
    slab, od, fit = couple_hbm.shape
    roots, width = trial_hbm.shape[1:]
    span = slab // od
    slots = pairs_hbm.shape[0]
    sends, rest = rest[: span - 1], rest[span - 1 :]
    (first_w, second_w, trials, levels, pairs, counts, blocks, occ, shift, own_ints, pair_ints, couple, trial, vir,
     own_w, pair_w, total, x_levels, inverse, sems) = rest
    me = lax.axis_index("aux")
    near = [lax.rem(me + ahead, ndomain) for ahead in range(span)]
    wanted = [(pairs_hbm, pairs), (counts_hbm, counts), (blocks_hbm, blocks), (vir_hbm, vir), (occ_hbm, occ),
              (shift_hbm, shift), (couple_hbm, couple)]
    wanted += [(trial_hbm.at[pl.ds(near[ahead] * od, od)], trial.at[ahead]) for ahead in range(span)]
    wanted += [(ints_hbm.at[row], own_ints.at[row]) for row in range(od)]
    copies = [pltpu.make_async_copy(source, target, sems.at[at]) for at, (source, target) in enumerate(wanted)]
    got_pairs, got_counts, got_blocks, got_vir, got_occ, got_shift, got_couple = copies[:7]
    got_trial, got_own = copies[7 : 7 + span], copies[7 + span :]
    for copy in copies:
        copy.start()
    total[...] = jnp.zeros_like(total)

    def where(slot):
        second = pairs[slot, 1, me]
        ahead = lax.rem(lax.div(second, od) - me + ndomain, ndomain)
        return ahead, pairs[slot, 0, me] - me * od, ahead * od + lax.rem(second, od)

    def second_ints(slot):
        return pltpu.make_async_copy(
            ints_hbm.at[where(slot)[2]], pair_ints.at[slot], sems.at[len(copies) + slot]
        )

    got_pairs.wait()
    for slot in range(sure):
        second_ints(slot).start()
    got_counts.wait()
    count = counts[me]
    for slot in range(sure, slots):
        pl.when(count > slot)(lambda slot=slot: second_ints(slot).start())
    got_blocks.wait()
    got_vir.wait()
    for ahead in range(span):
        levels[ahead] = jnp.concatenate(
            [vir[pl.ds(blocks[part, near[ahead]], 1), :] for part in range(blocks.shape[0])], axis=1
        )
    x_levels[...] = column(levels[0])
    got_occ.wait()
    got_shift.wait()

    def prepare(slot):
        invert(
            inverse.at[slot], x_levels, levels[where(slot)[0]],
            root_shifts(pairs, occ, shift, slot, me, roots),
        )

    for slot in range(sure):
        prepare(slot)
    for slot in range(sure, slots):
        pl.when(count > slot)(lambda slot=slot: prepare(slot))
    for ahead in range(span):
        got_trial[ahead].wait()
        trials[ahead] = jnp.concatenate([trial[ahead, l].astype(F32) for l in range(od)], axis=0)
    got_couple.wait()
    couplings = jnp.concatenate([couple[row].astype(F32) for row in range(slab)], axis=0).astype(BF16)
    for row in range(od):
        got_own[row].wait()
        found = jnp.dot(couplings, own_ints[row], preferred_element_type=F32)
        for other in range(od, slab):
            own_w[row, other] = found[other * od : (other + 1) * od]

    def weigh(slot):
        second_ints(slot).wait()
        found = jnp.dot(couplings, pair_ints[slot], preferred_element_type=F32)
        for other in range(od):
            pair_w[slot, other] = found[other * od : (other + 1) * od]

    def add(slot):
        ahead, row_i, row_j = where(slot)
        first_w[slot] = own_w[row_i, row_j]
        second_w[slot] = pair_w[slot, row_i]
        found = contract(
            roots, trials[0], first_w[slot], trials[ahead], second_w[slot], inverse[slot]
        )
        total[ahead] += jnp.where(count > slot, found, 0.0)

    for slot in range(sure):
        weigh(slot)
    for slot in range(sure):
        add(slot)
    for slot in range(sure, slots):

        @pl.when(count > slot)
        def _(slot=slot):
            weigh(slot)
            add(slot)

    for ahead, send in enumerate(sends):
        for l in range(od):
            send[l] = total[ahead + 1, l * roots : (l + 1) * roots]


def keep_kernel(
    ndomain, pairs_hbm, counts_hbm, occ_hbm, shift_hbm, first_w, second_w, trials, levels, kept,
    pairs, counts, occ, shift, total, x_levels, inverse, sems,
):
    span, rows, width = trials.shape
    od = first_w.shape[1]
    roots = rows // od
    me = lax.axis_index("aux")
    small = [
        pltpu.make_async_copy(source, target, sems.at[at])
        for at, (source, target) in enumerate(
            [(pairs_hbm, pairs), (counts_hbm, counts), (occ_hbm, occ), (shift_hbm, shift)]
        )
    ]
    for copy in small:
        copy.start()
    total[...] = jnp.zeros_like(total)
    for ahead in range(span):
        x_levels[ahead] = column(levels[ahead])
    for copy in small:
        copy.wait()

    @pl.loop(0, counts[me])
    def _(slot):
        ahead = lax.rem(lax.div(pairs[slot, 1, me], od) - me + ndomain, ndomain)
        invert(inverse, x_levels.at[ahead], levels[0], root_shifts(pairs, occ, shift, slot, me, roots))
        total[...] += contract(
            roots, trials[ahead], second_w[slot], trials[0], first_w[slot], inverse[...]
        )

    for l in range(od):
        kept[l] = total[l * roots : (l + 1) * roots]


def per_device(
    ints_ov, ints_oo, trial, occ_energy, vir_energy, root_shift, vir_blocks, pair_list, pair_count
):
    slab, od, fit = ints_oo.shape
    roots, width = trial.shape[1:]
    ndomain = lax.axis_size("aux")
    span = slab // od
    level_table = vir_energy.reshape(-1, LANES)
    pairs = jnp.transpose(pair_list, (1, 2, 0))
    blocks = vir_blocks.T
    hbm = pl.BlockSpec(memory_space=pltpu.HBM)
    vmem = pl.BlockSpec(memory_space=pltpu.VMEM)
    part = jax.ShapeDtypeStruct((od, roots, width), F32)
    params = pltpu.CompilerParams(vmem_limit_bytes=40 * 1024 * 1024)
    scalars = [pltpu.SMEM(x.shape, x.dtype) for x in (pairs, pair_count, blocks, occ_energy, root_shift)]
    def stay(*arrays):
        return [pltpu.with_memory_space_constraint(array, pltpu.HBM) for array in arrays]

    slots = pair_list.shape[1]
    sure = min(2, slots)
    *sends, first_w, second_w, trials, levels = pl.pallas_call(
        functools.partial(send_kernel, ndomain, sure),
        out_shape=[part] * (span - 1)
        + [
            jax.ShapeDtypeStruct((slots, od, width), F32),
            jax.ShapeDtypeStruct((slots, od, width), F32),
            jax.ShapeDtypeStruct((span, od * roots, width), F32),
            jax.ShapeDtypeStruct((span, 1, width), F32),
        ],
        in_specs=[hbm] * 9,
        out_specs=[vmem] * (span + 3),
        scratch_shapes=scalars
        + [
            pltpu.VMEM((od, fit, width), BF16),
            pltpu.VMEM((slots, fit, width), BF16),
            pltpu.VMEM(ints_oo.shape, BF16),
            pltpu.VMEM((span, od, roots, width), BF16),
            pltpu.VMEM(level_table.shape, F32),
            pltpu.VMEM((od, slab, od, width), F32),
            pltpu.VMEM((slots, od, od, width), F32),
            pltpu.VMEM((span, od * roots, width), F32),
            pltpu.VMEM((width, LANES), F32),
            pltpu.VMEM((slots, roots * width, width), BF16),
            pltpu.SemaphoreType.DMA((7 + span + od + slots,)),
        ],
        compiler_params=params,
        name="to_send",
    )(*stay(pairs, pair_count, blocks, occ_energy, root_shift, ints_ov, ints_oo, trial, level_table))
    arrived = [passed_along(send, "aux", at + 1) for at, send in enumerate(sends)]
    kept = pl.pallas_call(
        functools.partial(keep_kernel, ndomain),
        out_shape=part,
        in_specs=[hbm] * 4 + [vmem] * 4,
        out_specs=vmem,
        scratch_shapes=scalars[:2]
        + scalars[3:]
        + [
            pltpu.VMEM((od * roots, width), F32),
            pltpu.VMEM((span, width, LANES), F32),
            pltpu.VMEM((roots * width, width), BF16),
            pltpu.SemaphoreType.DMA((4,)),
        ],
        compiler_params=params,
        cost_estimate=pl.CostEstimate(flops=10**9, bytes_accessed=10**6, transcendentals=10**6),
        name="to_keep",
    )(*stay(pairs, pair_count, occ_energy, root_shift), first_w, second_w, trials, levels)
    return functools.reduce(jnp.add, arrived, kept)


def solution(mesh):
    in_specs = (
        P(("job", "aux"), None, None),
        P(("job", "aux"), None, None),
        P("job", None, None),
        P("job"),
        P("job"),
        P("job"),
        P("job", None),
        P("job", None, None),
        P("job"),
    )
    out_specs = P(("job", "aux"), None, None)
    return jax.shard_map(
        per_device, mesh=mesh, in_specs=in_specs, out_specs=out_specs, check_vma=False
    )
```

```python
import functools

import jax
import jax.numpy as jnp
from jax import lax
from jax.experimental import pallas as pl
from jax.experimental.pallas import tpu as pltpu
from jax.sharding import PartitionSpec as P

F32, BF16 = jnp.float32, jnp.bfloat16
LANES = 128


def passed_along(value, axis, steps):
    count = lax.axis_size(axis)
    pairs = [(source, (source + steps[source % 2]) % count) for source in range(count)]
    return lax.ppermute(value, axis, pairs)


def plan_of(span, count):
    ahead = range(1, span)
    if count % 2:
        return [(steps, steps) for steps in ahead]
    odd = [steps for steps in ahead if steps % 2]
    return [(steps, steps) for steps in ahead if steps % 2 == 0] + list(zip(odd[::-1], odd))


def column(row):
    return jnp.concatenate(
        [
            jnp.broadcast_to(row[:, at : at + LANES], (LANES, LANES)).T
            for at in range(0, row.shape[1], LANES)
        ],
        axis=0,
    )


def spread(w, roots):
    return jnp.concatenate(
        [jnp.broadcast_to(w[l : l + 1], (roots, w.shape[1])) for l in range(w.shape[0])], axis=0
    )


def factors(trial, w, roots):
    od, width = w.shape
    by_trial = [
        jnp.concatenate([trial[l * roots : (l + 1) * roots]] * od, axis=0) for l in range(od)
    ]
    by_w = [jnp.broadcast_to(w[l : l + 1], (od * roots, width)) for l in range(od)]
    return by_trial, by_w


def root_shifts(pairs, occ, shift, slot, me, roots):
    energy = occ[pairs[slot, 0, me]] + occ[pairs[slot, 1, me]]
    return [energy + shift[k] for k in range(roots)]


def invert(target, x_levels, y_levels, shifts, step=64):
    width = y_levels.shape[1]
    roots = len(shifts)
    for k in range(0, roots, 2):
        for at in range(0, width, step):
            x_wide = jnp.concatenate([x_levels[at : at + step]] * (width // LANES), axis=1)
            one = x_wide + (y_levels - shifts[k])
            if k + 1 == roots:
                found = [pltpu.reciprocal(one, approx=True)]
            else:
                two = x_wide + (y_levels - shifts[k + 1])
                both = pltpu.reciprocal(one * two, approx=True)
                found = [both * two, both * one]
            for more, value in enumerate(found):
                start = (k + more) * width + at
                target[start : start + step] = value.astype(BF16)


def contract(roots, x_trial, x_w, y_trial, y_w, inverse):
    od, width = x_w.shape
    rows = od * roots
    x_by_trial, x_by_w = factors(x_trial, x_w, roots)
    y_by_trial, y_by_w = factors(y_trial, y_w, roots)
    weight = spread(x_w, roots)
    left = jnp.concatenate([part * weight for part in x_by_trial + x_by_w], axis=0)
    high = left.astype(BF16).astype(F32)
    left = jnp.concatenate([high, left - high], axis=0)
    root_of = lax.rem(lax.broadcasted_iota(jnp.int32, left.shape, 0), roots)
    left = jnp.concatenate(
        [jnp.where(root_of == k, left, 0.0).astype(BF16) for k in range(roots)], axis=1
    )
    summed = jnp.dot(left, inverse, preferred_element_type=F32)
    half = summed.shape[0] // 2
    summed = summed[:half] + summed[half:]
    parts = [
        summed[at * rows : (at + 1) * rows] * other for at, other in enumerate(y_by_w + y_by_trial)
    ]
    return functools.reduce(jnp.add, parts)


def send_kernel(
    ndomain, sure, plan, pairs_hbm, counts_hbm, blocks_hbm, occ_hbm, shift_hbm, ints_hbm, couple_hbm, trial_hbm, vir_hbm,
    *rest,
):
    slab, od, fit = couple_hbm.shape
    roots, width = trial_hbm.shape[1:]
    span = slab // od
    slots = pairs_hbm.shape[0]
    sends, rest = rest[: span - 1], rest[span - 1 :]
    (first_w, second_w, trials, levels, pairs, counts, blocks, occ, shift, own_ints, pair_ints, couple, trial, vir,
     own_w, pair_w, total, x_levels, inverse, sems) = rest
    me = lax.axis_index("aux")
    near = [lax.rem(me + ahead, ndomain) for ahead in range(span)]
    wanted = [(pairs_hbm, pairs), (counts_hbm, counts), (blocks_hbm, blocks), (vir_hbm, vir), (occ_hbm, occ),
              (shift_hbm, shift), (couple_hbm, couple)]
    wanted += [(trial_hbm.at[pl.ds(near[ahead] * od, od)], trial.at[ahead]) for ahead in range(span)]
    wanted += [(ints_hbm.at[row], own_ints.at[row]) for row in range(od)]
    copies = [pltpu.make_async_copy(source, target, sems.at[at]) for at, (source, target) in enumerate(wanted)]
    got_pairs, got_counts, got_blocks, got_vir, got_occ, got_shift, got_couple = copies[:7]
    got_trial, got_own = copies[7 : 7 + span], copies[7 + span :]
    for copy in copies:
        copy.start()
    total[...] = jnp.zeros_like(total)

    def where(slot):
        second = pairs[slot, 1, me]
        ahead = lax.rem(lax.div(second, od) - me + ndomain, ndomain)
        return ahead, pairs[slot, 0, me] - me * od, ahead * od + lax.rem(second, od)

    def second_ints(slot):
        return pltpu.make_async_copy(
            ints_hbm.at[where(slot)[2]], pair_ints.at[slot], sems.at[len(copies) + slot]
        )

    got_pairs.wait()
    for slot in range(sure):
        second_ints(slot).start()
    got_counts.wait()
    count = counts[me]
    for slot in range(sure, slots):
        pl.when(count > slot)(lambda slot=slot: second_ints(slot).start())
    got_blocks.wait()
    got_vir.wait()
    for ahead in range(span):
        levels[ahead] = jnp.concatenate(
            [vir[pl.ds(blocks[part, near[ahead]], 1), :] for part in range(blocks.shape[0])], axis=1
        )
    x_levels[...] = column(levels[0])
    got_occ.wait()
    got_shift.wait()

    def prepare(slot):
        invert(
            inverse.at[slot], x_levels, levels[where(slot)[0]],
            root_shifts(pairs, occ, shift, slot, me, roots),
        )

    for ahead in range(span):
        got_trial[ahead].wait()
        trials[ahead] = jnp.concatenate([trial[ahead, l].astype(F32) for l in range(od)], axis=0)
    got_couple.wait()
    couplings = jnp.concatenate([couple[row].astype(F32) for row in range(slab)], axis=0).astype(BF16)
    for copy in got_own:
        copy.wait()
    for row in range(od):
        found = jnp.dot(couplings, own_ints[row], preferred_element_type=F32)
        for other in range(od, slab):
            own_w[row, other] = found[other * od : (other + 1) * od]
    for slot in range(sure):
        prepare(slot)
    for slot in range(sure, slots):
        pl.when(count > slot)(lambda slot=slot: prepare(slot))

    def weigh(slot):
        second_ints(slot).wait()
        found = jnp.dot(couplings, pair_ints[slot], preferred_element_type=F32)
        for other in range(od):
            pair_w[slot, other] = found[other * od : (other + 1) * od]

    def add(slot):
        ahead, row_i, row_j = where(slot)
        first_w[slot] = own_w[row_i, row_j]
        second_w[slot] = pair_w[slot, row_i]
        found = contract(
            roots, trials[0], first_w[slot], trials[ahead], second_w[slot], inverse[slot]
        )
        total[ahead] += jnp.where(count > slot, found, 0.0)

    for slot in range(sure):
        weigh(slot)
    for slot in range(sure):
        add(slot)
    for slot in range(sure, slots):

        @pl.when(count > slot)
        def _(slot=slot):
            weigh(slot)
            add(slot)

    for (even, odd), send in zip(plan, sends):
        ahead = jnp.where(lax.rem(me, 2) == 0, even, odd)
        for l in range(od):
            send[l] = total[ahead, l * roots : (l + 1) * roots]


def keep_kernel(
    ndomain, pairs_hbm, counts_hbm, occ_hbm, shift_hbm, first_w, second_w, trials, levels, kept,
    pairs, counts, occ, shift, total, x_levels, inverse, sems,
):
    span, rows, width = trials.shape
    od = first_w.shape[1]
    roots = rows // od
    me = lax.axis_index("aux")
    small = [
        pltpu.make_async_copy(source, target, sems.at[at])
        for at, (source, target) in enumerate(
            [(pairs_hbm, pairs), (counts_hbm, counts), (occ_hbm, occ), (shift_hbm, shift)]
        )
    ]
    for copy in small:
        copy.start()
    total[...] = jnp.zeros_like(total)
    for ahead in range(1, span):
        x_levels[ahead] = column(levels[ahead])
    for copy in small:
        copy.wait()

    @pl.loop(0, counts[me])
    def _(slot):
        ahead = lax.rem(lax.div(pairs[slot, 1, me], od) - me + ndomain, ndomain)
        invert(inverse, x_levels.at[ahead], levels[0], root_shifts(pairs, occ, shift, slot, me, roots))
        total[...] += contract(
            roots, trials[ahead], second_w[slot], trials[0], first_w[slot], inverse[...]
        )

    for l in range(od):
        kept[l] = total[l * roots : (l + 1) * roots]


def per_device(
    ints_ov, ints_oo, trial, occ_energy, vir_energy, root_shift, vir_blocks, pair_list, pair_count
):
    slab, od, fit = ints_oo.shape
    roots, width = trial.shape[1:]
    ndomain = lax.axis_size("aux")
    span = slab // od
    level_table = vir_energy.reshape(-1, LANES)
    pairs = jnp.transpose(pair_list, (1, 2, 0))
    blocks = vir_blocks.T
    hbm = pl.BlockSpec(memory_space=pltpu.HBM)
    vmem = pl.BlockSpec(memory_space=pltpu.VMEM)
    part = jax.ShapeDtypeStruct((od, roots, width), F32)
    params = pltpu.CompilerParams(vmem_limit_bytes=40 * 1024 * 1024)
    scalars = [pltpu.SMEM(x.shape, x.dtype) for x in (pairs, pair_count, blocks, occ_energy, root_shift)]
    def stay(*arrays):
        return [pltpu.with_memory_space_constraint(array, pltpu.HBM) for array in arrays]

    slots = pair_list.shape[1]
    sure = min(2, slots)
    plan = plan_of(span, ndomain)
    *sends, first_w, second_w, trials, levels = pl.pallas_call(
        functools.partial(send_kernel, ndomain, sure, plan),
        out_shape=[part] * (span - 1)
        + [
            jax.ShapeDtypeStruct((slots, od, width), F32),
            jax.ShapeDtypeStruct((slots, od, width), F32),
            jax.ShapeDtypeStruct((span, od * roots, width), F32),
            jax.ShapeDtypeStruct((span, 1, width), F32),
        ],
        in_specs=[hbm] * 9,
        out_specs=[vmem] * (span + 3),
        scratch_shapes=scalars
        + [
            pltpu.VMEM((od, fit, width), BF16),
            pltpu.VMEM((slots, fit, width), BF16),
            pltpu.VMEM(ints_oo.shape, BF16),
            pltpu.VMEM((span, od, roots, width), BF16),
            pltpu.VMEM(level_table.shape, F32),
            pltpu.VMEM((od, slab, od, width), F32),
            pltpu.VMEM((slots, od, od, width), F32),
            pltpu.VMEM((span, od * roots, width), F32),
            pltpu.VMEM((width, LANES), F32),
            pltpu.VMEM((slots, roots * width, width), BF16),
            pltpu.SemaphoreType.DMA((7 + span + od + slots,)),
        ],
        compiler_params=params,
        name="to_send",
    )(*stay(pairs, pair_count, blocks, occ_energy, root_shift, ints_ov, ints_oo, trial, level_table))
    arrived = [passed_along(send, "aux", steps) for send, steps in zip(sends, plan)]
    kept = pl.pallas_call(
        functools.partial(keep_kernel, ndomain),
        out_shape=part,
        in_specs=[hbm] * 4 + [vmem] * 4,
        out_specs=vmem,
        scratch_shapes=scalars[:2]
        + scalars[3:]
        + [
            pltpu.VMEM((od * roots, width), F32),
            pltpu.VMEM((span, width, LANES), F32),
            pltpu.VMEM((roots * width, width), BF16),
            pltpu.SemaphoreType.DMA((4,)),
        ],
        compiler_params=params,
        cost_estimate=pl.CostEstimate(flops=10**9, bytes_accessed=10**6, transcendentals=10**6),
        name="to_keep",
    )(*stay(pairs, pair_count, occ_energy, root_shift), first_w, second_w, trials, levels)
    return functools.reduce(jnp.add, arrived, kept)


def solution(mesh):
    in_specs = (
        P(("job", "aux"), None, None),
        P(("job", "aux"), None, None),
        P("job", None, None),
        P("job"),
        P("job"),
        P("job"),
        P("job", None),
        P("job", None, None),
        P("job"),
    )
    out_specs = P(("job", "aux"), None, None)
    return jax.shard_map(
        per_device, mesh=mesh, in_specs=in_specs, out_specs=out_specs, check_vma=False
    )
```

```python
import functools

import jax
import jax.numpy as jnp
from jax import lax
from jax.experimental import pallas as pl
from jax.experimental.pallas import tpu as pltpu
from jax.sharding import PartitionSpec as P

F32, BF16 = jnp.float32, jnp.bfloat16
LANES = 128


def passed_along(value, axis, steps):
    count = lax.axis_size(axis)
    pairs = [(source, (source + steps[source % 2]) % count) for source in range(count)]
    return lax.ppermute(value, axis, pairs)


def plan_of(span, count):
    ahead = range(1, span)
    if count % 2:
        return [(steps, steps) for steps in ahead]
    odd = [steps for steps in ahead if steps % 2]
    return [(steps, steps) for steps in ahead if steps % 2 == 0] + list(zip(odd[::-1], odd))


def column(row):
    return jnp.concatenate(
        [
            jnp.broadcast_to(row[:, at : at + LANES], (LANES, LANES)).T
            for at in range(0, row.shape[1], LANES)
        ],
        axis=0,
    )


def spread(w, roots):
    return jnp.concatenate(
        [jnp.broadcast_to(w[l : l + 1], (roots, w.shape[1])) for l in range(w.shape[0])], axis=0
    )


def factors(trial, w, roots):
    od, width = w.shape
    by_trial = [
        jnp.concatenate([trial[l * roots : (l + 1) * roots]] * od, axis=0) for l in range(od)
    ]
    by_w = [jnp.broadcast_to(w[l : l + 1], (od * roots, width)) for l in range(od)]
    return by_trial, by_w


def root_shifts(pairs, occ, shift, slot, me, roots):
    energy = occ[pairs[slot, 0, me]] + occ[pairs[slot, 1, me]]
    return [energy + shift[k] for k in range(roots)]


def invert(target, x_levels, y_levels, shifts, step=64):
    width = y_levels.shape[1]
    roots = len(shifts)
    for k in range(0, roots, 2):
        for at in range(0, width, step):
            x_wide = jnp.concatenate([x_levels[at : at + step]] * (width // LANES), axis=1)
            one = x_wide + (y_levels - shifts[k])
            if k + 1 == roots:
                found = [pltpu.reciprocal(one, approx=True)]
            else:
                two = x_wide + (y_levels - shifts[k + 1])
                both = pltpu.reciprocal(one * two, approx=True)
                found = [both * two, both * one]
            for more, value in enumerate(found):
                start = (k + more) * width + at
                target[start : start + step] = value.astype(BF16)


def reduce_x(roots, x_trial, x_w, inverse):
    x_by_trial, x_by_w = factors(x_trial, x_w, roots)
    weight = spread(x_w, roots)
    left = jnp.concatenate([part * weight for part in x_by_trial + x_by_w], axis=0)
    high = left.astype(BF16).astype(F32)
    left = jnp.concatenate([high, left - high], axis=0)
    root_of = lax.rem(lax.broadcasted_iota(jnp.int32, left.shape, 0), roots)
    left = jnp.concatenate(
        [jnp.where(root_of == k, left, 0.0).astype(BF16) for k in range(roots)], axis=1
    )
    summed = jnp.dot(left, inverse, preferred_element_type=F32)
    half = summed.shape[0] // 2
    return summed[:half] + summed[half:]


def join_y(roots, reduced, y_trial, y_w):
    rows = y_w.shape[0] * roots
    y_by_trial, y_by_w = factors(y_trial, y_w, roots)
    parts = [
        reduced[at * rows : (at + 1) * rows] * other for at, other in enumerate(y_by_w + y_by_trial)
    ]
    return functools.reduce(jnp.add, parts)


def rows_of(trial, k):
    od, width = len(trial), trial[0].shape[1]
    return jnp.concatenate([jnp.broadcast_to(t[k : k + 1], (od, width)) for t in trial], axis=0)


def send_kernel(
    ndomain, sure, plan, pairs_hbm, counts_hbm, blocks_hbm, occ_hbm, shift_hbm, ints_hbm, couple_hbm, trial_hbm, vir_hbm,
    *rest,
):
    slab, od, fit = couple_hbm.shape
    roots, width = trial_hbm.shape[1:]
    span = slab // od
    slots = pairs_hbm.shape[0]
    sends, rest = rest[: span - 1], rest[span - 1 :]
    (first_w, second_w, trials, levels, pairs, counts, blocks, occ, shift, own_ints, pair_ints, couple, trial, vir,
     own_w, pair_w, reduced, total, x_form, y_form, x_levels, sems) = rest
    me = lax.axis_index("aux")
    near = [lax.rem(me + ahead, ndomain) for ahead in range(span)]
    wanted = [(pairs_hbm, pairs), (counts_hbm, counts), (blocks_hbm, blocks), (vir_hbm, vir), (occ_hbm, occ),
              (shift_hbm, shift), (couple_hbm, couple)]
    wanted += [(trial_hbm.at[pl.ds(near[ahead] * od, od)], trial.at[ahead]) for ahead in range(span)]
    wanted += [(ints_hbm.at[row], own_ints.at[row]) for row in range(od)]
    copies = [pltpu.make_async_copy(source, target, sems.at[at]) for at, (source, target) in enumerate(wanted)]
    got_pairs, got_counts, got_blocks, got_vir, got_occ, got_shift, got_couple = copies[:7]
    got_trial, got_own = copies[7 : 7 + span], copies[7 + span :]
    for copy in copies:
        copy.start()
    total[...] = jnp.zeros_like(total)

    def where(slot):
        second = pairs[slot, 1, me]
        ahead = lax.rem(lax.div(second, od) - me + ndomain, ndomain)
        return ahead, pairs[slot, 0, me] - me * od, ahead * od + lax.rem(second, od)

    def second_ints(slot):
        return pltpu.make_async_copy(
            ints_hbm.at[where(slot)[2]], pair_ints.at[slot], sems.at[len(copies) + slot]
        )

    got_pairs.wait()
    for slot in range(sure):
        second_ints(slot).start()
    got_counts.wait()
    count = counts[me]
    for slot in range(sure, slots):
        pl.when(count > slot)(lambda slot=slot: second_ints(slot).start())
    got_blocks.wait()
    got_vir.wait()
    for ahead in range(span):
        levels[ahead] = jnp.concatenate(
            [vir[pl.ds(blocks[part, near[ahead]], 1), :] for part in range(blocks.shape[0])], axis=1
        )
    x_levels[...] = column(levels[0])
    got_occ.wait()
    got_shift.wait()

    for ahead in range(span):
        got_trial[ahead].wait()
        mine = [trial[ahead, l].astype(F32) for l in range(od)]
        trials[ahead] = jnp.concatenate(mine, axis=0)
        unit = jnp.ones((od * od, width), F32)
        for k in range(roots):
            if ahead == 0:
                x_form[k] = jnp.concatenate([rows_of(mine, k), unit], axis=0)
            else:
                y_form[ahead, k] = jnp.concatenate([unit, rows_of(mine, k)], axis=0)
    got_couple.wait()
    couplings = jnp.concatenate([couple[row].astype(F32) for row in range(slab)], axis=0).astype(BF16)
    for copy in got_own:
        copy.wait()
    for row in range(od):
        found = jnp.dot(couplings, own_ints[row], preferred_element_type=F32)
        for other in range(od, slab):
            own_w[row, other] = found[other * od : (other + 1) * od]
    def gather(slot):
        _, row_i, row_j = where(slot)
        first_w[slot] = own_w[row_i, row_j]
        w = first_w[slot]
        by_l = jnp.concatenate([w] * od, axis=0)
        by_other = jnp.concatenate(
            [jnp.broadcast_to(w[l : l + 1], (od, width)) for l in range(od)], axis=0
        )
        scale = jnp.concatenate([by_l, by_other * by_l], axis=0)
        shifts = root_shifts(pairs, occ, shift, slot, me, roots)
        y_levels = levels[where(slot)[0]]
        x_wide = jnp.concatenate([x_levels[...]] * (width // LANES), axis=1)
        for k in range(roots):
            inverse = pltpu.reciprocal(x_wide + (y_levels - shifts[k]), approx=True).astype(BF16)
            left = x_form[k] * scale
            high = left.astype(BF16).astype(F32)
            left = jnp.concatenate([high, left - high], axis=0).astype(BF16)
            both = jnp.dot(left, inverse, preferred_element_type=F32)
            half = both.shape[0] // 2
            reduced[slot, k] = both[:half] + both[half:]

    def join(slot):
        ahead, row_i, _ = where(slot)
        w = pair_w[slot, row_i]
        second_w[slot] = w
        other = jnp.concatenate(
            [jnp.broadcast_to(w[l : l + 1], (od, width)) for l in range(od)]
            + [jnp.ones((od * od, width), F32)],
            axis=0,
        )
        other = jnp.where(count > slot, other, 0.0)
        for k in range(roots):
            total[ahead, k] += reduced[slot, k] * y_form[ahead, k] * other

    def weigh(slot):
        second_ints(slot).wait()
        found = jnp.dot(couplings, pair_ints[slot], preferred_element_type=F32)
        for other in range(od):
            pair_w[slot, other] = found[other * od : (other + 1) * od]

    for slot in range(sure):
        gather(slot)
    for slot in range(sure):
        weigh(slot)
    for slot in range(sure):
        join(slot)
    for slot in range(sure, slots):

        @pl.when(count > slot)
        def _(slot=slot):
            weigh(slot)
            gather(slot)
            join(slot)

    for (even, odd), send in zip(plan, sends):
        ahead = jnp.where(lax.rem(me, 2) == 0, even, odd)
        for k in range(roots):
            found = total[ahead, k]
            found = functools.reduce(
                jnp.add, [found[at : at + od] for at in range(0, found.shape[0], od)]
            )
            for l in range(od):
                send[l, k : k + 1] = found[l : l + 1]


def keep_kernel(
    ndomain, pairs_hbm, counts_hbm, occ_hbm, shift_hbm, first_w, second_w, trials, levels, kept,
    pairs, counts, occ, shift, total, x_levels, inverse, sems,
):
    span, rows, width = trials.shape
    od = first_w.shape[1]
    roots = rows // od
    me = lax.axis_index("aux")
    small = [
        pltpu.make_async_copy(source, target, sems.at[at])
        for at, (source, target) in enumerate(
            [(pairs_hbm, pairs), (counts_hbm, counts), (occ_hbm, occ), (shift_hbm, shift)]
        )
    ]
    for copy in small:
        copy.start()
    total[...] = jnp.zeros_like(total)
    for ahead in range(1, span):
        x_levels[ahead] = column(levels[ahead])
    for copy in small:
        copy.wait()

    @pl.loop(0, counts[me])
    def _(slot):
        ahead = lax.rem(lax.div(pairs[slot, 1, me], od) - me + ndomain, ndomain)
        invert(inverse, x_levels.at[ahead], levels[0], root_shifts(pairs, occ, shift, slot, me, roots))
        reduced = reduce_x(roots, trials[ahead], second_w[slot], inverse[...])
        total[...] += join_y(roots, reduced, trials[0], first_w[slot])

    for l in range(od):
        kept[l] = total[l * roots : (l + 1) * roots]


def per_device(
    ints_ov, ints_oo, trial, occ_energy, vir_energy, root_shift, vir_blocks, pair_list, pair_count
):
    slab, od, fit = ints_oo.shape
    roots, width = trial.shape[1:]
    ndomain = lax.axis_size("aux")
    span = slab // od
    level_table = vir_energy.reshape(-1, LANES)
    pairs = jnp.transpose(pair_list, (1, 2, 0))
    blocks = vir_blocks.T
    hbm = pl.BlockSpec(memory_space=pltpu.HBM)
    vmem = pl.BlockSpec(memory_space=pltpu.VMEM)
    part = jax.ShapeDtypeStruct((od, roots, width), F32)
    params = pltpu.CompilerParams(vmem_limit_bytes=40 * 1024 * 1024)
    scalars = [pltpu.SMEM(x.shape, x.dtype) for x in (pairs, pair_count, blocks, occ_energy, root_shift)]
    def stay(*arrays):
        return [pltpu.with_memory_space_constraint(array, pltpu.HBM) for array in arrays]

    slots = pair_list.shape[1]
    sure = min(2, slots)
    plan = plan_of(span, ndomain)
    *sends, first_w, second_w, trials, levels = pl.pallas_call(
        functools.partial(send_kernel, ndomain, sure, plan),
        out_shape=[part] * (span - 1)
        + [
            jax.ShapeDtypeStruct((slots, od, width), F32),
            jax.ShapeDtypeStruct((slots, od, width), F32),
            jax.ShapeDtypeStruct((span, od * roots, width), F32),
            jax.ShapeDtypeStruct((span, 1, width), F32),
        ],
        in_specs=[hbm] * 9,
        out_specs=[vmem] * (span + 3),
        scratch_shapes=scalars
        + [
            pltpu.VMEM((od, fit, width), BF16),
            pltpu.VMEM((slots, fit, width), BF16),
            pltpu.VMEM(ints_oo.shape, BF16),
            pltpu.VMEM((span, od, roots, width), BF16),
            pltpu.VMEM(level_table.shape, F32),
            pltpu.VMEM((od, slab, od, width), F32),
            pltpu.VMEM((slots, od, od, width), F32),
            pltpu.VMEM((slots, roots, 2 * od * od, width), F32),
            pltpu.VMEM((span, roots, 2 * od * od, width), F32),
            pltpu.VMEM((roots, 2 * od * od, width), F32),
            pltpu.VMEM((span, roots, 2 * od * od, width), F32),
            pltpu.VMEM((width, LANES), F32),
            pltpu.SemaphoreType.DMA((7 + span + od + slots,)),
        ],
        compiler_params=params,
        name="to_send",
    )(*stay(pairs, pair_count, blocks, occ_energy, root_shift, ints_ov, ints_oo, trial, level_table))
    arrived = [passed_along(send, "aux", steps) for send, steps in zip(sends, plan)]
    kept = pl.pallas_call(
        functools.partial(keep_kernel, ndomain),
        out_shape=part,
        in_specs=[hbm] * 4 + [vmem] * 4,
        out_specs=vmem,
        scratch_shapes=scalars[:2]
        + scalars[3:]
        + [
            pltpu.VMEM((od * roots, width), F32),
            pltpu.VMEM((span, width, LANES), F32),
            pltpu.VMEM((roots * width, width), BF16),
            pltpu.SemaphoreType.DMA((4,)),
        ],
        compiler_params=params,
        cost_estimate=pl.CostEstimate(flops=10**9, bytes_accessed=10**6, transcendentals=10**6),
        name="to_keep",
    )(*stay(pairs, pair_count, occ_energy, root_shift), first_w, second_w, trials, levels)
    return functools.reduce(jnp.add, arrived, kept)


def solution(mesh):
    in_specs = (
        P(("job", "aux"), None, None),
        P(("job", "aux"), None, None),
        P("job", None, None),
        P("job"),
        P("job"),
        P("job"),
        P("job", None),
        P("job", None, None),
        P("job"),
    )
    out_specs = P(("job", "aux"), None, None)
    return jax.shard_map(
        per_device, mesh=mesh, in_specs=in_specs, out_specs=out_specs, check_vma=False
    )
```

```python
import functools

import jax
import jax.numpy as jnp
from jax import lax
from jax.experimental import pallas as pl
from jax.experimental.pallas import tpu as pltpu
from jax.sharding import PartitionSpec as P

F32, BF16 = jnp.float32, jnp.bfloat16
LANES = 128


def passed_along(value, axis, steps):
    count = lax.axis_size(axis)
    pairs = [(source, (source + steps[source % 2]) % count) for source in range(count)]
    return lax.ppermute(value, axis, pairs)


def plan_of(span, count):
    ahead = range(1, span)
    if count % 2:
        return [(steps, steps) for steps in ahead]
    odd = [steps for steps in ahead if steps % 2]
    return [(steps, steps) for steps in ahead if steps % 2 == 0] + list(zip(odd[::-1], odd))


def column(row):
    return jnp.concatenate(
        [
            jnp.broadcast_to(row[:, at : at + LANES], (LANES, LANES)).T
            for at in range(0, row.shape[1], LANES)
        ],
        axis=0,
    )


def spread(w, roots):
    return jnp.concatenate(
        [jnp.broadcast_to(w[l : l + 1], (roots, w.shape[1])) for l in range(w.shape[0])], axis=0
    )


def factors(trial, w, roots):
    od, width = w.shape
    by_trial = [
        jnp.concatenate([trial[l * roots : (l + 1) * roots]] * od, axis=0) for l in range(od)
    ]
    by_w = [jnp.broadcast_to(w[l : l + 1], (od * roots, width)) for l in range(od)]
    return by_trial, by_w


def root_shifts(pairs, occ, shift, slot, me, roots):
    energy = occ[pairs[slot, 0, me]] + occ[pairs[slot, 1, me]]
    return [energy + shift[k] for k in range(roots)]


def invert(target, x_levels, y_levels, shifts, step=64):
    width = y_levels.shape[1]
    roots = len(shifts)
    for k in range(0, roots, 2):
        for at in range(0, width, step):
            x_wide = jnp.concatenate([x_levels[at : at + step]] * (width // LANES), axis=1)
            one = x_wide + (y_levels - shifts[k])
            if k + 1 == roots:
                found = [pltpu.reciprocal(one, approx=True)]
            else:
                two = x_wide + (y_levels - shifts[k + 1])
                both = pltpu.reciprocal(one * two, approx=True)
                found = [both * two, both * one]
            for more, value in enumerate(found):
                start = (k + more) * width + at
                target[start : start + step] = value.astype(BF16)


def reduce_x(roots, x_trial, x_w, inverse):
    x_by_trial, x_by_w = factors(x_trial, x_w, roots)
    weight = spread(x_w, roots)
    left = jnp.concatenate([part * weight for part in x_by_trial + x_by_w], axis=0)
    high = left.astype(BF16).astype(F32)
    left = jnp.concatenate([high, left - high], axis=0)
    root_of = lax.rem(lax.broadcasted_iota(jnp.int32, left.shape, 0), roots)
    left = jnp.concatenate(
        [jnp.where(root_of == k, left, 0.0).astype(BF16) for k in range(roots)], axis=1
    )
    summed = jnp.dot(left, inverse, preferred_element_type=F32)
    half = summed.shape[0] // 2
    return summed[:half] + summed[half:]


def join_y(roots, reduced, y_trial, y_w):
    rows = y_w.shape[0] * roots
    y_by_trial, y_by_w = factors(y_trial, y_w, roots)
    parts = [
        reduced[at * rows : (at + 1) * rows] * other for at, other in enumerate(y_by_w + y_by_trial)
    ]
    return functools.reduce(jnp.add, parts)


def rows_of(trial, k):
    od, width = len(trial), trial[0].shape[1]
    return jnp.concatenate([jnp.broadcast_to(t[k : k + 1], (od, width)) for t in trial], axis=0)


def send_kernel(
    ndomain, sure, plan, pairs_hbm, counts_hbm, blocks_hbm, occ_hbm, shift_hbm, ints_hbm, couple_hbm, trial_hbm, vir_hbm,
    *rest,
):
    slab, od, fit = couple_hbm.shape
    roots, width = trial_hbm.shape[1:]
    span = slab // od
    slots = pairs_hbm.shape[0]
    sends, rest = rest[: span - 1], rest[span - 1 :]
    (first_w, second_w, trials, levels, pairs, counts, blocks, occ, shift, ints, couple, trial, vir,
     own_w, pair_w, reduced, total, x_form, y_form, x_levels, sems) = rest
    me = lax.axis_index("aux")
    near = [lax.rem(me + ahead, ndomain) for ahead in range(span)]
    wanted = [(pairs_hbm, pairs), (counts_hbm, counts), (blocks_hbm, blocks), (vir_hbm, vir), (occ_hbm, occ),
              (shift_hbm, shift), (couple_hbm, couple)]
    wanted += [(trial_hbm, trial)]
    wanted += [(ints_hbm.at[pl.ds(0, od)], ints.at[pl.ds(0, od)]), (ints_hbm.at[pl.ds(od, slab - od)], ints.at[pl.ds(od, slab - od)])]
    copies = [pltpu.make_async_copy(source, target, sems.at[at]) for at, (source, target) in enumerate(wanted)]
    got_pairs, got_counts, got_blocks, got_vir, got_occ, got_shift, got_couple = copies[:7]
    got_trial, got_own, *got_rest = copies[7:]
    for copy in copies:
        copy.start()
    total[...] = jnp.zeros_like(total)

    def where(slot):
        second = pairs[slot, 1, me]
        ahead = lax.rem(lax.div(second, od) - me + ndomain, ndomain)
        return ahead, pairs[slot, 0, me] - me * od, ahead * od + lax.rem(second, od)

    got_pairs.wait()
    got_counts.wait()
    count = counts[me]
    got_blocks.wait()
    got_vir.wait()
    for ahead in range(span):
        levels[ahead] = jnp.concatenate(
            [vir[pl.ds(blocks[part, near[ahead]], 1), :] for part in range(blocks.shape[0])], axis=1
        )
    x_levels[...] = column(levels[0])
    got_occ.wait()
    got_shift.wait()

    got_trial.wait()
    for ahead in range(span):
        mine = [trial[near[ahead] * od + l].astype(F32) for l in range(od)]
        trials[ahead] = jnp.concatenate(mine, axis=0)
        unit = jnp.ones((od * od, width), F32)
        for k in range(roots):
            if ahead == 0:
                x_form[k] = jnp.concatenate([rows_of(mine, k), unit], axis=0)
            else:
                y_form[ahead, k] = jnp.concatenate([unit, rows_of(mine, k)], axis=0)
    got_couple.wait()
    couplings = jnp.concatenate([couple[row].astype(F32) for row in range(slab)], axis=0).astype(BF16)
    got_own.wait()
    for row in range(od):
        found = jnp.dot(couplings, ints[row], preferred_element_type=F32)
        for other in range(od, slab):
            own_w[row, other] = found[other * od : (other + 1) * od]
    def gather(slot):
        _, row_i, row_j = where(slot)
        first_w[slot] = own_w[row_i, row_j]
        w = first_w[slot]
        by_l = jnp.concatenate([w] * od, axis=0)
        by_other = jnp.concatenate(
            [jnp.broadcast_to(w[l : l + 1], (od, width)) for l in range(od)], axis=0
        )
        scale = jnp.concatenate([by_l, by_other * by_l], axis=0)
        shifts = root_shifts(pairs, occ, shift, slot, me, roots)
        y_levels = levels[where(slot)[0]]
        x_wide = jnp.concatenate([x_levels[...]] * (width // LANES), axis=1)
        for k in range(roots):
            inverse = pltpu.reciprocal(x_wide + (y_levels - shifts[k]), approx=True).astype(BF16)
            left = x_form[k] * scale
            high = left.astype(BF16).astype(F32)
            left = jnp.concatenate([high, left - high], axis=0).astype(BF16)
            both = jnp.dot(left, inverse, preferred_element_type=F32)
            half = both.shape[0] // 2
            reduced[slot, k] = both[:half] + both[half:]

    def join(slot):
        ahead, row_i, _ = where(slot)
        w = pair_w[slot, row_i]
        second_w[slot] = w
        other = jnp.concatenate(
            [jnp.broadcast_to(w[l : l + 1], (od, width)) for l in range(od)]
            + [jnp.ones((od * od, width), F32)],
            axis=0,
        )
        other = jnp.where(count > slot, other, 0.0)
        for k in range(roots):
            total[ahead, k] += reduced[slot, k] * y_form[ahead, k] * other

    def weigh(slot):
        found = jnp.dot(couplings, ints[where(slot)[2]], preferred_element_type=F32)
        for other in range(od):
            pair_w[slot, other] = found[other * od : (other + 1) * od]

    for slot in range(sure):
        gather(slot)
    for copy in got_rest:
        copy.wait()
    for slot in range(sure):
        weigh(slot)
    for slot in range(sure):
        join(slot)
    for slot in range(sure, slots):

        @pl.when(count > slot)
        def _(slot=slot):
            weigh(slot)
            gather(slot)
            join(slot)

    for (even, odd), send in zip(plan, sends):
        ahead = jnp.where(lax.rem(me, 2) == 0, even, odd)
        for k in range(roots):
            found = total[ahead, k]
            found = functools.reduce(
                jnp.add, [found[at : at + od] for at in range(0, found.shape[0], od)]
            )
            for l in range(od):
                send[l, k : k + 1] = found[l : l + 1]


def keep_kernel(
    ndomain, pairs_hbm, counts_hbm, occ_hbm, shift_hbm, first_w, second_w, trials, levels, kept,
    pairs, counts, occ, shift, total, x_levels, inverse, sems,
):
    span, rows, width = trials.shape
    od = first_w.shape[1]
    roots = rows // od
    me = lax.axis_index("aux")
    small = [
        pltpu.make_async_copy(source, target, sems.at[at])
        for at, (source, target) in enumerate(
            [(pairs_hbm, pairs), (counts_hbm, counts), (occ_hbm, occ), (shift_hbm, shift)]
        )
    ]
    for copy in small:
        copy.start()
    total[...] = jnp.zeros_like(total)
    for ahead in range(1, span):
        x_levels[ahead] = column(levels[ahead])
    for copy in small:
        copy.wait()

    @pl.loop(0, counts[me])
    def _(slot):
        ahead = lax.rem(lax.div(pairs[slot, 1, me], od) - me + ndomain, ndomain)
        invert(inverse, x_levels.at[ahead], levels[0], root_shifts(pairs, occ, shift, slot, me, roots))
        reduced = reduce_x(roots, trials[ahead], second_w[slot], inverse[...])
        total[...] += join_y(roots, reduced, trials[0], first_w[slot])

    for l in range(od):
        kept[l] = total[l * roots : (l + 1) * roots]


def per_device(
    ints_ov, ints_oo, trial, occ_energy, vir_energy, root_shift, vir_blocks, pair_list, pair_count
):
    slab, od, fit = ints_oo.shape
    roots, width = trial.shape[1:]
    ndomain = lax.axis_size("aux")
    span = slab // od
    level_table = vir_energy.reshape(-1, LANES)
    pairs = jnp.transpose(pair_list, (1, 2, 0))
    blocks = vir_blocks.T
    hbm = pl.BlockSpec(memory_space=pltpu.HBM)
    vmem = pl.BlockSpec(memory_space=pltpu.VMEM)
    part = jax.ShapeDtypeStruct((od, roots, width), F32)
    params = pltpu.CompilerParams(vmem_limit_bytes=40 * 1024 * 1024)
    scalars = [pltpu.SMEM(x.shape, x.dtype) for x in (pairs, pair_count, blocks, occ_energy, root_shift)]
    def stay(*arrays):
        return [pltpu.with_memory_space_constraint(array, pltpu.HBM) for array in arrays]

    slots = pair_list.shape[1]
    sure = min(2, slots)
    plan = plan_of(span, ndomain)
    *sends, first_w, second_w, trials, levels = pl.pallas_call(
        functools.partial(send_kernel, ndomain, sure, plan),
        out_shape=[part] * (span - 1)
        + [
            jax.ShapeDtypeStruct((slots, od, width), F32),
            jax.ShapeDtypeStruct((slots, od, width), F32),
            jax.ShapeDtypeStruct((span, od * roots, width), F32),
            jax.ShapeDtypeStruct((span, 1, width), F32),
        ],
        in_specs=[hbm] * 9,
        out_specs=[vmem] * (span + 3),
        scratch_shapes=scalars
        + [
            pltpu.VMEM(ints_ov.shape, BF16),
            pltpu.VMEM(ints_oo.shape, BF16),
            pltpu.VMEM(trial.shape, BF16),
            pltpu.VMEM(level_table.shape, F32),
            pltpu.VMEM((od, slab, od, width), F32),
            pltpu.VMEM((slots, od, od, width), F32),
            pltpu.VMEM((slots, roots, 2 * od * od, width), F32),
            pltpu.VMEM((span, roots, 2 * od * od, width), F32),
            pltpu.VMEM((roots, 2 * od * od, width), F32),
            pltpu.VMEM((span, roots, 2 * od * od, width), F32),
            pltpu.VMEM((width, LANES), F32),
            pltpu.SemaphoreType.DMA((10,)),
        ],
        compiler_params=params,
        name="to_send",
    )(*stay(pairs, pair_count, blocks, occ_energy, root_shift, ints_ov, ints_oo, trial, level_table))
    arrived = [passed_along(send, "aux", steps) for send, steps in zip(sends, plan)]
    kept = pl.pallas_call(
        functools.partial(keep_kernel, ndomain),
        out_shape=part,
        in_specs=[hbm] * 4 + [vmem] * 4,
        out_specs=vmem,
        scratch_shapes=scalars[:2]
        + scalars[3:]
        + [
            pltpu.VMEM((od * roots, width), F32),
            pltpu.VMEM((span, width, LANES), F32),
            pltpu.VMEM((roots * width, width), BF16),
            pltpu.SemaphoreType.DMA((4,)),
        ],
        compiler_params=params,
        cost_estimate=pl.CostEstimate(flops=10**9, bytes_accessed=10**6, transcendentals=10**6),
        name="to_keep",
    )(*stay(pairs, pair_count, occ_energy, root_shift), first_w, second_w, trials, levels)
    return functools.reduce(jnp.add, arrived, kept)


def solution(mesh):
    in_specs = (
        P(("job", "aux"), None, None),
        P(("job", "aux"), None, None),
        P("job", None, None),
        P("job"),
        P("job"),
        P("job"),
        P("job", None),
        P("job", None, None),
        P("job"),
    )
    out_specs = P(("job", "aux"), None, None)
    return jax.shard_map(
        per_device, mesh=mesh, in_specs=in_specs, out_specs=out_specs, check_vma=False
    )
```

```python
import functools

import jax
import jax.numpy as jnp
from jax import lax
from jax.experimental import pallas as pl
from jax.experimental.pallas import tpu as pltpu
from jax.sharding import PartitionSpec as P

F32, BF16 = jnp.float32, jnp.bfloat16
LANES = 128


def passed_along(value, axis, steps):
    count = lax.axis_size(axis)
    pairs = [(source, (source + steps[source % 2]) % count) for source in range(count)]
    return lax.ppermute(value, axis, pairs)


def plan_of(span, count):
    ahead = range(1, span)
    if count % 2:
        return [(steps, steps) for steps in ahead]
    odd = [steps for steps in ahead if steps % 2]
    return [(steps, steps) for steps in ahead if steps % 2 == 0] + list(zip(odd[::-1], odd))


def column(row):
    return jnp.concatenate(
        [
            jnp.broadcast_to(row[:, at : at + LANES], (LANES, LANES)).T
            for at in range(0, row.shape[1], LANES)
        ],
        axis=0,
    )


def spread(w, roots):
    return jnp.concatenate(
        [jnp.broadcast_to(w[l : l + 1], (roots, w.shape[1])) for l in range(w.shape[0])], axis=0
    )


def root_shifts(pairs, occ, shift, slot, me, roots):
    energy = occ[pairs[slot, 0, me]] + occ[pairs[slot, 1, me]]
    return [energy + shift[k] for k in range(roots)]


def rows_of(trial, k):
    od, width = len(trial), trial[0].shape[1]
    return jnp.concatenate([jnp.broadcast_to(t[k : k + 1], (od, width)) for t in trial], axis=0)


def sum_over_x(form, w, x_levels, y_levels, shifts):
    od, width = w.shape
    by_l = jnp.concatenate([w] * od, axis=0)
    scale = jnp.concatenate([by_l, spread(w, od) * by_l], axis=0)
    x_wide = jnp.concatenate([x_levels] * (width // LANES), axis=1)
    results = []
    for k, shift in enumerate(shifts):
        inverse = pltpu.reciprocal(x_wide + (y_levels - shift), approx=True).astype(BF16)
        left = form[k] * scale
        high = left.astype(BF16).astype(F32)
        left = jnp.concatenate([high, left - high], axis=0).astype(BF16)
        both = jnp.dot(left, inverse, preferred_element_type=F32)
        half = both.shape[0] // 2
        results.append(both[:half] + both[half:])
    return results


def fold(summed, od):
    return functools.reduce(jnp.add, [summed[at : at + od] for at in range(0, summed.shape[0], od)])


def send_kernel(
    ndomain, sure, plan, pairs_hbm, counts_hbm, blocks_hbm, occ_hbm, shift_hbm, ints_hbm, couple_hbm, trial_hbm, vir_hbm,
    *rest,
):
    slab, od, fit = couple_hbm.shape
    roots, width = trial_hbm.shape[1:]
    span = slab // od
    slots = pairs_hbm.shape[0]
    sends, rest = rest[: span - 1], rest[span - 1 :]
    (first_w, second_w, trials, levels, pairs, counts, blocks, occ, shift, ints, couple, trial, vir,
     own_w, pair_w, reduced, total, x_form, y_form, x_levels, sems) = rest
    me = lax.axis_index("aux")
    near = [lax.rem(me + ahead, ndomain) for ahead in range(span)]
    wanted = [(pairs_hbm, pairs), (counts_hbm, counts), (blocks_hbm, blocks), (vir_hbm, vir), (occ_hbm, occ),
              (shift_hbm, shift), (couple_hbm, couple)]
    wanted += [(trial_hbm, trial)]
    wanted += [(ints_hbm.at[pl.ds(0, od)], ints.at[pl.ds(0, od)]), (ints_hbm.at[pl.ds(od, slab - od)], ints.at[pl.ds(od, slab - od)])]
    copies = [pltpu.make_async_copy(source, target, sems.at[at]) for at, (source, target) in enumerate(wanted)]
    got_pairs, got_counts, got_blocks, got_vir, got_occ, got_shift, got_couple = copies[:7]
    got_trial, got_own, *got_rest = copies[7:]
    for copy in copies:
        copy.start()
    total[...] = jnp.zeros_like(total)

    def where(slot):
        second = pairs[slot, 1, me]
        ahead = lax.rem(lax.div(second, od) - me + ndomain, ndomain)
        return ahead, pairs[slot, 0, me] - me * od, ahead * od + lax.rem(second, od)

    got_pairs.wait()
    got_counts.wait()
    count = counts[me]
    got_blocks.wait()
    got_vir.wait()
    for ahead in range(span):
        levels[ahead] = jnp.concatenate(
            [vir[pl.ds(blocks[part, near[ahead]], 1), :] for part in range(blocks.shape[0])], axis=1
        )
    x_levels[...] = column(levels[0])
    got_occ.wait()
    got_shift.wait()

    got_trial.wait()
    for ahead in range(span):
        mine = [trial[near[ahead] * od + l].astype(F32) for l in range(od)]
        trials[ahead] = jnp.concatenate(mine, axis=0)
        unit = jnp.ones((od * od, width), F32)
        for k in range(roots):
            if ahead == 0:
                x_form[k] = jnp.concatenate([rows_of(mine, k), unit], axis=0)
            else:
                y_form[ahead, k] = jnp.concatenate([unit, rows_of(mine, k)], axis=0)
    got_couple.wait()
    couplings = jnp.concatenate([couple[row].astype(F32) for row in range(slab)], axis=0).astype(BF16)
    got_own.wait()
    for row in range(od):
        found = jnp.dot(couplings, ints[row], preferred_element_type=F32)
        for other in range(od, slab):
            own_w[row, other] = found[other * od : (other + 1) * od]
    def gather(slot):
        _, row_i, row_j = where(slot)
        first_w[slot] = own_w[row_i, row_j]
        found = sum_over_x(
            x_form, first_w[slot], x_levels[...], levels[where(slot)[0]],
            root_shifts(pairs, occ, shift, slot, me, roots),
        )
        for k in range(roots):
            reduced[slot, k] = found[k]

    def join(slot):
        ahead, row_i, _ = where(slot)
        w = pair_w[slot, row_i]
        second_w[slot] = w
        other = jnp.concatenate(
            [spread(w, od), jnp.ones((od * od, width), F32)], axis=0
        )
        other = jnp.where(count > slot, other, 0.0)
        for k in range(roots):
            total[ahead, k] += reduced[slot, k] * y_form[ahead, k] * other

    def weigh(slot):
        found = jnp.dot(couplings, ints[where(slot)[2]], preferred_element_type=F32)
        for other in range(od):
            pair_w[slot, other] = found[other * od : (other + 1) * od]

    for slot in range(sure):
        gather(slot)
    for copy in got_rest:
        copy.wait()
    for slot in range(sure):
        weigh(slot)
    for slot in range(sure):
        join(slot)
    for slot in range(sure, slots):

        @pl.when(count > slot)
        def _(slot=slot):
            weigh(slot)
            gather(slot)
            join(slot)

    for (even, odd), send in zip(plan, sends):
        ahead = jnp.where(lax.rem(me, 2) == 0, even, odd)
        for k in range(roots):
            found = fold(total[ahead, k], od)
            for l in range(od):
                send[l, k : k + 1] = found[l : l + 1]


def keep_kernel(
    ndomain, pairs_hbm, counts_hbm, occ_hbm, shift_hbm, first_w, second_w, trials, levels, kept,
    pairs, counts, occ, shift, total, x_form, y_form, x_levels, sems,
):
    span, rows, width = trials.shape
    od = first_w.shape[1]
    roots = rows // od
    me = lax.axis_index("aux")
    small = [
        pltpu.make_async_copy(source, target, sems.at[at])
        for at, (source, target) in enumerate(
            [(pairs_hbm, pairs), (counts_hbm, counts), (occ_hbm, occ), (shift_hbm, shift)]
        )
    ]
    for copy in small:
        copy.start()
    total[...] = jnp.zeros_like(total)
    unit = jnp.ones((od * od, width), F32)
    for ahead in range(span):
        mine = [trials[ahead, l * roots : (l + 1) * roots] for l in range(od)]
        for k in range(roots):
            if ahead == 0:
                y_form[k] = jnp.concatenate([unit, rows_of(mine, k)], axis=0)
            else:
                x_form[ahead, k] = jnp.concatenate([rows_of(mine, k), unit], axis=0)
        if ahead > 0:
            x_levels[ahead] = column(levels[ahead])
    for copy in small:
        copy.wait()

    @pl.loop(0, counts[me])
    def _(slot):
        ahead = lax.rem(lax.div(pairs[slot, 1, me], od) - me + ndomain, ndomain)
        found = sum_over_x(
            x_form.at[ahead], second_w[slot], x_levels[ahead], levels[0],
            root_shifts(pairs, occ, shift, slot, me, roots),
        )
        other = jnp.concatenate([spread(first_w[slot], od), unit], axis=0)
        for k in range(roots):
            total[k] += found[k] * y_form[k] * other

    for k in range(roots):
        found = fold(total[k], od)
        for l in range(od):
            kept[l, k : k + 1] = found[l : l + 1]


def per_device(
    ints_ov, ints_oo, trial, occ_energy, vir_energy, root_shift, vir_blocks, pair_list, pair_count
):
    slab, od, fit = ints_oo.shape
    roots, width = trial.shape[1:]
    ndomain = lax.axis_size("aux")
    span = slab // od
    level_table = vir_energy.reshape(-1, LANES)
    pairs = jnp.transpose(pair_list, (1, 2, 0))
    blocks = vir_blocks.T
    hbm = pl.BlockSpec(memory_space=pltpu.HBM)
    vmem = pl.BlockSpec(memory_space=pltpu.VMEM)
    part = jax.ShapeDtypeStruct((od, roots, width), F32)
    params = pltpu.CompilerParams(vmem_limit_bytes=40 * 1024 * 1024)
    scalars = [pltpu.SMEM(x.shape, x.dtype) for x in (pairs, pair_count, blocks, occ_energy, root_shift)]
    def stay(*arrays):
        return [pltpu.with_memory_space_constraint(array, pltpu.HBM) for array in arrays]

    slots = pair_list.shape[1]
    sure = min(2, slots)
    plan = plan_of(span, ndomain)
    *sends, first_w, second_w, trials, levels = pl.pallas_call(
        functools.partial(send_kernel, ndomain, sure, plan),
        out_shape=[part] * (span - 1)
        + [
            jax.ShapeDtypeStruct((slots, od, width), F32),
            jax.ShapeDtypeStruct((slots, od, width), F32),
            jax.ShapeDtypeStruct((span, od * roots, width), F32),
            jax.ShapeDtypeStruct((span, 1, width), F32),
        ],
        in_specs=[hbm] * 9,
        out_specs=[vmem] * (span + 3),
        scratch_shapes=scalars
        + [
            pltpu.VMEM(ints_ov.shape, BF16),
            pltpu.VMEM(ints_oo.shape, BF16),
            pltpu.VMEM(trial.shape, BF16),
            pltpu.VMEM(level_table.shape, F32),
            pltpu.VMEM((od, slab, od, width), F32),
            pltpu.VMEM((slots, od, od, width), F32),
            pltpu.VMEM((slots, roots, 2 * od * od, width), F32),
            pltpu.VMEM((span, roots, 2 * od * od, width), F32),
            pltpu.VMEM((roots, 2 * od * od, width), F32),
            pltpu.VMEM((span, roots, 2 * od * od, width), F32),
            pltpu.VMEM((width, LANES), F32),
            pltpu.SemaphoreType.DMA((10,)),
        ],
        compiler_params=params,
        name="to_send",
    )(*stay(pairs, pair_count, blocks, occ_energy, root_shift, ints_ov, ints_oo, trial, level_table))
    arrived = [passed_along(send, "aux", steps) for send, steps in zip(sends, plan)]
    kept = pl.pallas_call(
        functools.partial(keep_kernel, ndomain),
        out_shape=part,
        in_specs=[hbm] * 4 + [vmem] * 4,
        out_specs=vmem,
        scratch_shapes=scalars[:2]
        + scalars[3:]
        + [
            pltpu.VMEM((roots, 2 * od * od, width), F32),
            pltpu.VMEM((span, roots, 2 * od * od, width), F32),
            pltpu.VMEM((roots, 2 * od * od, width), F32),
            pltpu.VMEM((span, width, LANES), F32),
            pltpu.SemaphoreType.DMA((4,)),
        ],
        compiler_params=params,
        cost_estimate=pl.CostEstimate(flops=10**9, bytes_accessed=10**6, transcendentals=10**6),
        name="to_keep",
    )(*stay(pairs, pair_count, occ_energy, root_shift), first_w, second_w, trials, levels)
    return functools.reduce(jnp.add, arrived, kept)


def solution(mesh):
    in_specs = (
        P(("job", "aux"), None, None),
        P(("job", "aux"), None, None),
        P("job", None, None),
        P("job"),
        P("job"),
        P("job"),
        P("job", None),
        P("job", None, None),
        P("job"),
    )
    out_specs = P(("job", "aux"), None, None)
    return jax.shard_map(
        per_device, mesh=mesh, in_specs=in_specs, out_specs=out_specs, check_vma=False
    )
```

```python
import functools

import jax
import jax.numpy as jnp
from jax import lax
from jax.experimental import pallas as pl
from jax.experimental.pallas import tpu as pltpu
from jax.sharding import PartitionSpec as P

F32, BF16 = jnp.float32, jnp.bfloat16
LANES = 128


def passed_along(value, axis, steps):
    count = lax.axis_size(axis)
    pairs = [(source, (source + steps[source % 2]) % count) for source in range(count)]
    return lax.ppermute(value, axis, pairs)


def plan_of(span, count):
    ahead = range(1, span)
    if count % 2:
        return [(steps, steps) for steps in ahead]
    odd = [steps for steps in ahead if steps % 2]
    return [(steps, steps) for steps in ahead if steps % 2 == 0] + list(zip(odd[::-1], odd))


def column(row):
    return jnp.concatenate(
        [
            jnp.broadcast_to(row[:, at : at + LANES], (LANES, LANES)).T
            for at in range(0, row.shape[1], LANES)
        ],
        axis=0,
    )


def spread(w, roots):
    return jnp.concatenate(
        [jnp.broadcast_to(w[l : l + 1], (roots, w.shape[1])) for l in range(w.shape[0])], axis=0
    )


def factors(trial, w, roots):
    od, width = w.shape
    by_trial = [
        jnp.concatenate([trial[l * roots : (l + 1) * roots]] * od, axis=0) for l in range(od)
    ]
    by_w = [jnp.broadcast_to(w[l : l + 1], (od * roots, width)) for l in range(od)]
    return by_trial, by_w


def root_shifts(pairs, occ, shift, slot, me, roots):
    energy = occ[pairs[slot, 0, me]] + occ[pairs[slot, 1, me]]
    return [energy + shift[k] for k in range(roots)]


def invert(target, x_levels, y_levels, shifts, step=64):
    width = y_levels.shape[1]
    roots = len(shifts)
    for k in range(0, roots, 2):
        for at in range(0, width, step):
            x_wide = jnp.concatenate([x_levels[at : at + step]] * (width // LANES), axis=1)
            one = x_wide + (y_levels - shifts[k])
            if k + 1 == roots:
                found = [pltpu.reciprocal(one, approx=True)]
            else:
                two = x_wide + (y_levels - shifts[k + 1])
                both = pltpu.reciprocal(one * two, approx=True)
                found = [both * two, both * one]
            for more, value in enumerate(found):
                start = (k + more) * width + at
                target[start : start + step] = value.astype(BF16)


def reduce_x(roots, x_trial, x_w, inverse):
    x_by_trial, x_by_w = factors(x_trial, x_w, roots)
    weight = spread(x_w, roots)
    left = jnp.concatenate([part * weight for part in x_by_trial + x_by_w], axis=0)
    high = left.astype(BF16).astype(F32)
    left = jnp.concatenate([high, left - high], axis=0)
    root_of = lax.rem(lax.broadcasted_iota(jnp.int32, left.shape, 0), roots)
    left = jnp.concatenate(
        [jnp.where(root_of == k, left, 0.0).astype(BF16) for k in range(roots)], axis=1
    )
    summed = jnp.dot(left, inverse, preferred_element_type=F32)
    half = summed.shape[0] // 2
    return summed[:half] + summed[half:]


def join_y(roots, reduced, y_trial, y_w):
    rows = y_w.shape[0] * roots
    y_by_trial, y_by_w = factors(y_trial, y_w, roots)
    parts = [
        reduced[at * rows : (at + 1) * rows] * other for at, other in enumerate(y_by_w + y_by_trial)
    ]
    return functools.reduce(jnp.add, parts)


def rows_of(trial, k):
    od, width = len(trial), trial[0].shape[1]
    return jnp.concatenate([jnp.broadcast_to(t[k : k + 1], (od, width)) for t in trial], axis=0)


def send_kernel(
    ndomain, sure, plan, pairs_hbm, counts_hbm, blocks_hbm, occ_hbm, shift_hbm, ints_hbm, couple_hbm, trial_hbm, vir_hbm,
    *rest,
):
    slab, od, fit = couple_hbm.shape
    roots, width = trial_hbm.shape[1:]
    span = slab // od
    slots = pairs_hbm.shape[0]
    sends, rest = rest[: span - 1], rest[span - 1 :]
    (first_w, second_w, trials, levels, pairs, counts, blocks, occ, shift, ints, couple, trial, vir,
     own_w, pair_w, reduced, total, x_form, y_form, x_levels, sems) = rest
    me = lax.axis_index("aux")
    near = [lax.rem(me + ahead, ndomain) for ahead in range(span)]
    wanted = [(pairs_hbm, pairs), (counts_hbm, counts), (blocks_hbm, blocks), (vir_hbm, vir), (occ_hbm, occ),
              (shift_hbm, shift), (couple_hbm, couple)]
    wanted += [(trial_hbm, trial)]
    wanted += [(ints_hbm.at[pl.ds(0, od)], ints.at[pl.ds(0, od)]), (ints_hbm.at[pl.ds(od, slab - od)], ints.at[pl.ds(od, slab - od)])]
    copies = [pltpu.make_async_copy(source, target, sems.at[at]) for at, (source, target) in enumerate(wanted)]
    got_pairs, got_counts, got_blocks, got_vir, got_occ, got_shift, got_couple = copies[:7]
    got_trial, got_own, *got_rest = copies[7:]
    for copy in copies:
        copy.start()
    total[...] = jnp.zeros_like(total)

    def where(slot):
        second = pairs[slot, 1, me]
        ahead = lax.rem(lax.div(second, od) - me + ndomain, ndomain)
        return ahead, pairs[slot, 0, me] - me * od, ahead * od + lax.rem(second, od)

    got_pairs.wait()
    got_counts.wait()
    count = counts[me]
    got_blocks.wait()
    got_vir.wait()
    for ahead in range(span):
        levels[ahead] = jnp.concatenate(
            [vir[pl.ds(blocks[part, near[ahead]], 1), :] for part in range(blocks.shape[0])], axis=1
        )
    x_levels[...] = column(levels[0])
    got_occ.wait()
    got_shift.wait()

    got_trial.wait()
    for ahead in range(span):
        mine = [trial[near[ahead] * od + l].astype(F32) for l in range(od)]
        trials[ahead] = jnp.concatenate(mine, axis=0)
        unit = jnp.ones((od * od, width), F32)
        for k in range(roots):
            if ahead == 0:
                x_form[k] = jnp.concatenate([rows_of(mine, k), unit], axis=0)
            else:
                y_form[ahead, k] = jnp.concatenate([unit, rows_of(mine, k)], axis=0)
    got_couple.wait()
    couplings = jnp.concatenate([couple[row].astype(F32) for row in range(slab)], axis=0).astype(BF16)
    got_own.wait()
    for row in range(od):
        found = jnp.dot(couplings, ints[row], preferred_element_type=F32)
        for other in range(od, slab):
            own_w[row, other] = found[other * od : (other + 1) * od]
    def gather(slot):
        _, row_i, row_j = where(slot)
        first_w[slot] = own_w[row_i, row_j]
        w = first_w[slot]
        by_l = jnp.concatenate([w] * od, axis=0)
        by_other = jnp.concatenate(
            [jnp.broadcast_to(w[l : l + 1], (od, width)) for l in range(od)], axis=0
        )
        scale = jnp.concatenate([by_l, by_other * by_l], axis=0)
        shifts = root_shifts(pairs, occ, shift, slot, me, roots)
        y_levels = levels[where(slot)[0]]
        x_wide = jnp.concatenate([x_levels[...]] * (width // LANES), axis=1)
        made = []
        for k in range(roots):
            one = x_wide + (y_levels - shifts[k])
            if k == 0 and roots > 1:
                two = x_wide + (y_levels - shifts[k + 1])
                both = pltpu.reciprocal(one * two, approx=True)
                made += [(both * two).astype(BF16), (both * one).astype(BF16)]
            elif k != 1:
                made.append(pltpu.reciprocal(one, approx=True).astype(BF16))
        for k in range(roots):
            inverse = made[k]
            left = x_form[k] * scale
            high = left.astype(BF16).astype(F32)
            left = jnp.concatenate([high, left - high], axis=0).astype(BF16)
            both = jnp.dot(left, inverse, preferred_element_type=F32)
            half = both.shape[0] // 2
            reduced[slot, k] = both[:half] + both[half:]

    def join(slot):
        ahead, row_i, _ = where(slot)
        w = pair_w[slot, row_i]
        second_w[slot] = w
        other = jnp.concatenate(
            [jnp.broadcast_to(w[l : l + 1], (od, width)) for l in range(od)]
            + [jnp.ones((od * od, width), F32)],
            axis=0,
        )
        other = jnp.where(count > slot, other, 0.0)
        for k in range(roots):
            total[ahead, k] += reduced[slot, k] * y_form[ahead, k] * other

    def weigh(slot):
        found = jnp.dot(couplings, ints[where(slot)[2]], preferred_element_type=F32)
        for other in range(od):
            pair_w[slot, other] = found[other * od : (other + 1) * od]

    for slot in range(sure):
        gather(slot)
    for copy in got_rest:
        copy.wait()
    for slot in range(sure):
        weigh(slot)
    for slot in range(sure):
        join(slot)
    for slot in range(sure, slots):

        @pl.when(count > slot)
        def _(slot=slot):
            weigh(slot)
            gather(slot)
            join(slot)

    for (even, odd), send in zip(plan, sends):
        ahead = jnp.where(lax.rem(me, 2) == 0, even, odd)
        for k in range(roots):
            found = total[ahead, k]
            found = functools.reduce(
                jnp.add, [found[at : at + od] for at in range(0, found.shape[0], od)]
            )
            for l in range(od):
                send[l, k : k + 1] = found[l : l + 1]


def keep_kernel(
    ndomain, pairs_hbm, counts_hbm, occ_hbm, shift_hbm, first_w, second_w, trials, levels, kept,
    pairs, counts, occ, shift, total, x_levels, inverse, sems,
):
    span, rows, width = trials.shape
    od = first_w.shape[1]
    roots = rows // od
    me = lax.axis_index("aux")
    small = [
        pltpu.make_async_copy(source, target, sems.at[at])
        for at, (source, target) in enumerate(
            [(pairs_hbm, pairs), (counts_hbm, counts), (occ_hbm, occ), (shift_hbm, shift)]
        )
    ]
    for copy in small:
        copy.start()
    total[...] = jnp.zeros_like(total)
    for ahead in range(1, span):
        x_levels[ahead] = column(levels[ahead])
    for copy in small:
        copy.wait()

    @pl.loop(0, counts[me])
    def _(slot):
        ahead = lax.rem(lax.div(pairs[slot, 1, me], od) - me + ndomain, ndomain)
        invert(inverse, x_levels.at[ahead], levels[0], root_shifts(pairs, occ, shift, slot, me, roots))
        reduced = reduce_x(roots, trials[ahead], second_w[slot], inverse[...])
        total[...] += join_y(roots, reduced, trials[0], first_w[slot])

    for l in range(od):
        kept[l] = total[l * roots : (l + 1) * roots]


def per_device(
    ints_ov, ints_oo, trial, occ_energy, vir_energy, root_shift, vir_blocks, pair_list, pair_count
):
    slab, od, fit = ints_oo.shape
    roots, width = trial.shape[1:]
    ndomain = lax.axis_size("aux")
    span = slab // od
    level_table = vir_energy.reshape(-1, LANES)
    pairs = jnp.transpose(pair_list, (1, 2, 0))
    blocks = vir_blocks.T
    hbm = pl.BlockSpec(memory_space=pltpu.HBM)
    vmem = pl.BlockSpec(memory_space=pltpu.VMEM)
    part = jax.ShapeDtypeStruct((od, roots, width), F32)
    params = pltpu.CompilerParams(vmem_limit_bytes=40 * 1024 * 1024)
    scalars = [pltpu.SMEM(x.shape, x.dtype) for x in (pairs, pair_count, blocks, occ_energy, root_shift)]
    def stay(*arrays):
        return [pltpu.with_memory_space_constraint(array, pltpu.HBM) for array in arrays]

    slots = pair_list.shape[1]
    sure = min(2, slots)
    plan = plan_of(span, ndomain)
    *sends, first_w, second_w, trials, levels = pl.pallas_call(
        functools.partial(send_kernel, ndomain, sure, plan),
        out_shape=[part] * (span - 1)
        + [
            jax.ShapeDtypeStruct((slots, od, width), F32),
            jax.ShapeDtypeStruct((slots, od, width), F32),
            jax.ShapeDtypeStruct((span, od * roots, width), F32),
            jax.ShapeDtypeStruct((span, 1, width), F32),
        ],
        in_specs=[hbm] * 9,
        out_specs=[vmem] * (span + 3),
        scratch_shapes=scalars
        + [
            pltpu.VMEM(ints_ov.shape, BF16),
            pltpu.VMEM(ints_oo.shape, BF16),
            pltpu.VMEM(trial.shape, BF16),
            pltpu.VMEM(level_table.shape, F32),
            pltpu.VMEM((od, slab, od, width), F32),
            pltpu.VMEM((slots, od, od, width), F32),
            pltpu.VMEM((slots, roots, 2 * od * od, width), F32),
            pltpu.VMEM((span, roots, 2 * od * od, width), F32),
            pltpu.VMEM((roots, 2 * od * od, width), F32),
            pltpu.VMEM((span, roots, 2 * od * od, width), F32),
            pltpu.VMEM((width, LANES), F32),
            pltpu.SemaphoreType.DMA((10,)),
        ],
        compiler_params=params,
        name="to_send",
    )(*stay(pairs, pair_count, blocks, occ_energy, root_shift, ints_ov, ints_oo, trial, level_table))
    arrived = [passed_along(send, "aux", steps) for send, steps in zip(sends, plan)]
    kept = pl.pallas_call(
        functools.partial(keep_kernel, ndomain),
        out_shape=part,
        in_specs=[hbm] * 4 + [vmem] * 4,
        out_specs=vmem,
        scratch_shapes=scalars[:2]
        + scalars[3:]
        + [
            pltpu.VMEM((od * roots, width), F32),
            pltpu.VMEM((span, width, LANES), F32),
            pltpu.VMEM((roots * width, width), BF16),
            pltpu.SemaphoreType.DMA((4,)),
        ],
        compiler_params=params,
        cost_estimate=pl.CostEstimate(flops=10**9, bytes_accessed=10**6, transcendentals=10**6),
        name="to_keep",
    )(*stay(pairs, pair_count, occ_energy, root_shift), first_w, second_w, trials, levels)
    return functools.reduce(jnp.add, arrived, kept)


def solution(mesh):
    in_specs = (
        P(("job", "aux"), None, None),
        P(("job", "aux"), None, None),
        P("job", None, None),
        P("job"),
        P("job"),
        P("job"),
        P("job", None),
        P("job", None, None),
        P("job"),
    )
    out_specs = P(("job", "aux"), None, None)
    return jax.shard_map(
        per_device, mesh=mesh, in_specs=in_specs, out_specs=out_specs, check_vma=False
    )
```

```python
import functools

import jax
import jax.numpy as jnp
from jax import lax
from jax.experimental import pallas as pl
from jax.experimental.pallas import tpu as pltpu
from jax.sharding import PartitionSpec as P

F32, BF16 = jnp.float32, jnp.bfloat16
LANES = 128


def passed_along(value, axis, steps):
    count = lax.axis_size(axis)
    pairs = [(source, (source + steps[source % 2]) % count) for source in range(count)]
    return lax.ppermute(value, axis, pairs)


def plan_of(span, count):
    ahead = range(1, span)
    if count % 2:
        return [(steps, steps) for steps in ahead]
    odd = [steps for steps in ahead if steps % 2]
    return [(steps, steps) for steps in ahead if steps % 2 == 0] + list(zip(odd[::-1], odd))


def column(row):
    return jnp.concatenate(
        [
            jnp.broadcast_to(row[:, at : at + LANES], (LANES, LANES)).T
            for at in range(0, row.shape[1], LANES)
        ],
        axis=0,
    )


def spread(w, roots):
    return jnp.concatenate(
        [jnp.broadcast_to(w[l : l + 1], (roots, w.shape[1])) for l in range(w.shape[0])], axis=0
    )


def root_shifts(pairs, occ, shift, slot, me, roots):
    energy = occ[pairs[slot, 0, me]] + occ[pairs[slot, 1, me]]
    return [energy + shift[k] for k in range(roots)]


def rows_of(trial, k):
    od, width = len(trial), trial[0].shape[1]
    return jnp.concatenate([jnp.broadcast_to(t[k : k + 1], (od, width)) for t in trial], axis=0)


def sum_over_x(form, w, x_levels, y_levels, shifts):
    od, width = w.shape
    by_l = jnp.concatenate([w] * od, axis=0)
    scale = jnp.concatenate([by_l, spread(w, od) * by_l], axis=0)
    x_wide = jnp.concatenate([x_levels] * (width // LANES), axis=1)
    results = []
    ones = [x_wide + (y_levels - shift) for shift in shifts]
    shared = pltpu.reciprocal(ones[0] * ones[1], approx=True) if len(ones) > 1 else None
    for k, one in enumerate(ones):
        if k < 2 and shared is not None:
            inverse = (shared * ones[1 - k]).astype(BF16)
        else:
            inverse = pltpu.reciprocal(one, approx=True).astype(BF16)
        left = form[k] * scale
        high = left.astype(BF16).astype(F32)
        left = jnp.concatenate([high, left - high], axis=0).astype(BF16)
        both = jnp.dot(left, inverse, preferred_element_type=F32)
        half = both.shape[0] // 2
        results.append(both[:half] + both[half:])
    return results


def fold(summed, od):
    return functools.reduce(jnp.add, [summed[at : at + od] for at in range(0, summed.shape[0], od)])


def send_kernel(
    ndomain, sure, plan, pairs_hbm, counts_hbm, blocks_hbm, occ_hbm, shift_hbm, ints_hbm, couple_hbm, trial_hbm, vir_hbm,
    *rest,
):
    slab, od, fit = couple_hbm.shape
    roots, width = trial_hbm.shape[1:]
    span = slab // od
    slots = pairs_hbm.shape[0]
    sends, rest = rest[: span - 1], rest[span - 1 :]
    (first_w, second_w, trials, levels, pairs, counts, blocks, occ, shift, ints, couple, trial, vir,
     own_w, pair_w, reduced, total, x_form, y_form, x_levels, sems) = rest
    me = lax.axis_index("aux")
    near = [lax.rem(me + ahead, ndomain) for ahead in range(span)]
    wanted = [(pairs_hbm, pairs), (counts_hbm, counts), (blocks_hbm, blocks), (vir_hbm, vir), (occ_hbm, occ),
              (shift_hbm, shift), (couple_hbm, couple)]
    wanted += [(trial_hbm, trial)]
    wanted += [(ints_hbm.at[pl.ds(0, od)], ints.at[pl.ds(0, od)]), (ints_hbm.at[pl.ds(od, slab - od)], ints.at[pl.ds(od, slab - od)])]
    copies = [pltpu.make_async_copy(source, target, sems.at[at]) for at, (source, target) in enumerate(wanted)]
    got_pairs, got_counts, got_blocks, got_vir, got_occ, got_shift, got_couple = copies[:7]
    got_trial, got_own, *got_rest = copies[7:]
    for copy in copies:
        copy.start()
    total[...] = jnp.zeros_like(total)

    def where(slot):
        second = pairs[slot, 1, me]
        ahead = lax.rem(lax.div(second, od) - me + ndomain, ndomain)
        return ahead, pairs[slot, 0, me] - me * od, ahead * od + lax.rem(second, od)

    got_pairs.wait()
    got_counts.wait()
    count = counts[me]
    got_blocks.wait()
    got_vir.wait()
    for ahead in range(span):
        levels[ahead] = jnp.concatenate(
            [vir[pl.ds(blocks[part, near[ahead]], 1), :] for part in range(blocks.shape[0])], axis=1
        )
    x_levels[...] = column(levels[0])
    got_occ.wait()
    got_shift.wait()

    got_trial.wait()
    for ahead in range(span):
        mine = [trial[near[ahead] * od + l].astype(F32) for l in range(od)]
        trials[ahead] = jnp.concatenate(mine, axis=0)
        unit = jnp.ones((od * od, width), F32)
        for k in range(roots):
            if ahead == 0:
                x_form[k] = jnp.concatenate([rows_of(mine, k), unit], axis=0)
            else:
                y_form[ahead, k] = jnp.concatenate([unit, rows_of(mine, k)], axis=0)
    got_couple.wait()
    couplings = jnp.concatenate([couple[row].astype(F32) for row in range(slab)], axis=0).astype(BF16)
    got_own.wait()
    for row in range(od):
        found = jnp.dot(couplings, ints[row], preferred_element_type=F32)
        for other in range(od, slab):
            own_w[row, other] = found[other * od : (other + 1) * od]
    def gather(slot):
        _, row_i, row_j = where(slot)
        first_w[slot] = own_w[row_i, row_j]
        found = sum_over_x(
            x_form, first_w[slot], x_levels[...], levels[where(slot)[0]],
            root_shifts(pairs, occ, shift, slot, me, roots),
        )
        for k in range(roots):
            reduced[slot, k] = found[k]

    def join(slot):
        ahead, row_i, _ = where(slot)
        w = pair_w[slot, row_i]
        second_w[slot] = w
        other = jnp.concatenate(
            [spread(w, od), jnp.ones((od * od, width), F32)], axis=0
        )
        other = jnp.where(count > slot, other, 0.0)
        for k in range(roots):
            total[ahead, k] += reduced[slot, k] * y_form[ahead, k] * other

    def weigh(slot):
        found = jnp.dot(couplings, ints[where(slot)[2]], preferred_element_type=F32)
        for other in range(od):
            pair_w[slot, other] = found[other * od : (other + 1) * od]

    for slot in range(sure):
        gather(slot)
    for copy in got_rest:
        copy.wait()
    for slot in range(sure):
        weigh(slot)
    for slot in range(sure):
        join(slot)
    for slot in range(sure, slots):

        @pl.when(count > slot)
        def _(slot=slot):
            weigh(slot)
            gather(slot)
            join(slot)

    for (even, odd), send in zip(plan, sends):
        ahead = jnp.where(lax.rem(me, 2) == 0, even, odd)
        for k in range(roots):
            found = fold(total[ahead, k], od)
            for l in range(od):
                send[l, k : k + 1] = found[l : l + 1]


def keep_kernel(
    ndomain, pairs_hbm, counts_hbm, occ_hbm, shift_hbm, first_w, second_w, trials, levels, kept,
    pairs, counts, occ, shift, total, x_form, y_form, x_levels, sems,
):
    span, rows, width = trials.shape
    od = first_w.shape[1]
    roots = rows // od
    me = lax.axis_index("aux")
    small = [
        pltpu.make_async_copy(source, target, sems.at[at])
        for at, (source, target) in enumerate(
            [(pairs_hbm, pairs), (counts_hbm, counts), (occ_hbm, occ), (shift_hbm, shift)]
        )
    ]
    for copy in small:
        copy.start()
    total[...] = jnp.zeros_like(total)
    unit = jnp.ones((od * od, width), F32)
    for ahead in range(span):
        mine = [trials[ahead, l * roots : (l + 1) * roots] for l in range(od)]
        for k in range(roots):
            if ahead == 0:
                y_form[k] = jnp.concatenate([unit, rows_of(mine, k)], axis=0)
            else:
                x_form[ahead, k] = jnp.concatenate([rows_of(mine, k), unit], axis=0)
        if ahead > 0:
            x_levels[ahead] = column(levels[ahead])
    for copy in small:
        copy.wait()

    @pl.loop(0, counts[me])
    def _(slot):
        ahead = lax.rem(lax.div(pairs[slot, 1, me], od) - me + ndomain, ndomain)
        found = sum_over_x(
            x_form.at[ahead], second_w[slot], x_levels[ahead], levels[0],
            root_shifts(pairs, occ, shift, slot, me, roots),
        )
        other = jnp.concatenate([spread(first_w[slot], od), unit], axis=0)
        for k in range(roots):
            total[k] += found[k] * y_form[k] * other

    for k in range(roots):
        found = fold(total[k], od)
        for l in range(od):
            kept[l, k : k + 1] = found[l : l + 1]


def per_device(
    ints_ov, ints_oo, trial, occ_energy, vir_energy, root_shift, vir_blocks, pair_list, pair_count
):
    slab, od, fit = ints_oo.shape
    roots, width = trial.shape[1:]
    ndomain = lax.axis_size("aux")
    span = slab // od
    level_table = vir_energy.reshape(-1, LANES)
    pairs = jnp.transpose(pair_list, (1, 2, 0))
    blocks = vir_blocks.T
    hbm = pl.BlockSpec(memory_space=pltpu.HBM)
    vmem = pl.BlockSpec(memory_space=pltpu.VMEM)
    part = jax.ShapeDtypeStruct((od, roots, width), F32)
    params = pltpu.CompilerParams(vmem_limit_bytes=40 * 1024 * 1024)
    scalars = [pltpu.SMEM(x.shape, x.dtype) for x in (pairs, pair_count, blocks, occ_energy, root_shift)]
    def stay(*arrays):
        return [pltpu.with_memory_space_constraint(array, pltpu.HBM) for array in arrays]

    slots = pair_list.shape[1]
    sure = min(2, slots)
    plan = plan_of(span, ndomain)
    *sends, first_w, second_w, trials, levels = pl.pallas_call(
        functools.partial(send_kernel, ndomain, sure, plan),
        out_shape=[part] * (span - 1)
        + [
            jax.ShapeDtypeStruct((slots, od, width), F32),
            jax.ShapeDtypeStruct((slots, od, width), F32),
            jax.ShapeDtypeStruct((span, od * roots, width), F32),
            jax.ShapeDtypeStruct((span, 1, width), F32),
        ],
        in_specs=[hbm] * 9,
        out_specs=[vmem] * (span + 3),
        scratch_shapes=scalars
        + [
            pltpu.VMEM(ints_ov.shape, BF16),
            pltpu.VMEM(ints_oo.shape, BF16),
            pltpu.VMEM(trial.shape, BF16),
            pltpu.VMEM(level_table.shape, F32),
            pltpu.VMEM((od, slab, od, width), F32),
            pltpu.VMEM((slots, od, od, width), F32),
            pltpu.VMEM((slots, roots, 2 * od * od, width), F32),
            pltpu.VMEM((span, roots, 2 * od * od, width), F32),
            pltpu.VMEM((roots, 2 * od * od, width), F32),
            pltpu.VMEM((span, roots, 2 * od * od, width), F32),
            pltpu.VMEM((width, LANES), F32),
            pltpu.SemaphoreType.DMA((10,)),
        ],
        compiler_params=params,
        name="to_send",
    )(*stay(pairs, pair_count, blocks, occ_energy, root_shift, ints_ov, ints_oo, trial, level_table))
    arrived = [passed_along(send, "aux", steps) for send, steps in zip(sends, plan)]
    kept = pl.pallas_call(
        functools.partial(keep_kernel, ndomain),
        out_shape=part,
        in_specs=[hbm] * 4 + [vmem] * 4,
        out_specs=vmem,
        scratch_shapes=scalars[:2]
        + scalars[3:]
        + [
            pltpu.VMEM((roots, 2 * od * od, width), F32),
            pltpu.VMEM((span, roots, 2 * od * od, width), F32),
            pltpu.VMEM((roots, 2 * od * od, width), F32),
            pltpu.VMEM((span, width, LANES), F32),
            pltpu.SemaphoreType.DMA((4,)),
        ],
        compiler_params=params,
        cost_estimate=pl.CostEstimate(flops=10**9, bytes_accessed=10**6, transcendentals=10**6),
        name="to_keep",
    )(*stay(pairs, pair_count, occ_energy, root_shift), first_w, second_w, trials, levels)
    return functools.reduce(jnp.add, arrived, kept)


def solution(mesh):
    in_specs = (
        P(("job", "aux"), None, None),
        P(("job", "aux"), None, None),
        P("job", None, None),
        P("job"),
        P("job"),
        P("job"),
        P("job", None),
        P("job", None, None),
        P("job"),
    )
    out_specs = P(("job", "aux"), None, None)
    return jax.shard_map(
        per_device, mesh=mesh, in_specs=in_specs, out_specs=out_specs, check_vma=False
    )
```
